32 devices in a mesh: fsdp: 32 (over z, y, x, core).
Axes of the slice: x: 2, y: 2, z: 4, core: 2. Of those that a mesh axis runs over, the one named last changes fastest.
Arguments:
- tokens: bfloat16 [65536, 768], P('fsdp'), may hold values from -6 to 6
- qkv_weight: bfloat16 [1769472], P('fsdp'), may hold values from -0.21875 to 0.21875
- out_weight: bfloat16 [589824], P('fsdp'), may hold values from -1.75 to 1.75
- in_weight: bfloat16 [1769472], P('fsdp'), may hold values from -0.21875 to 0.21875
- mlp_weight: bfloat16 [884736], P('fsdp'), may hold values from -0.375 to 0.375
- norm_gains: bfloat16 [1536], P('fsdp'), may hold values from 0.5 to 1.5
- cotangent: bfloat16 [65536, 768], P('fsdp'), may hold values from -6 to 6
Outputs:
- mixed_output: bfloat16 [65536, 768], P('fsdp')
- tokens_grad: float32 [65536, 768], P('fsdp')
- qkv_weight_grad: float32 [1769472], P('fsdp')
- out_weight_grad: float32 [589824], P('fsdp')
- in_weight_grad: float32 [1769472], P('fsdp')
- mlp_weight_grad: float32 [884736], P('fsdp')
- norm_gains_grad: float32 [1536], P('fsdp')
The draws below stay inside these ranges and needn't reach their ends.
All inputs are finite; a program needn't handle non-finite values.
Results may differ from the reference program's by a relative error of at most 0.014.
Values may be sent and summed in bfloat16 or wider, within the bound.
No kernel may reach another device: no remote copies, remote signals or barrier semaphores. Data moves between devices by JAX's collectives and lax.ppermute only.
A program may use at most 256 MiB of HBM per device.

```python
import math
import jax
import jax.numpy as jnp
from jax import lax

D = 768
HEADS = 12
HEAD = 64
FF = 1152
WIN = 128
LEN = 512
TOKENS = 65536


def spiked(drawn, key, source, target, shards_of, factor):
    owner, partner = [(jnp.arange(drawn.shape[position]) // (drawn.shape[position] // shards_of)).reshape([-1 if axis == position else 1 for axis in range(drawn.ndim)]) for position in (source, target)]
    chosen = jax.random.permutation(key, shards_of)[partner]
    strong = (owner == chosen) | (owner == (partner + shards_of // 2) % shards_of)
    return jnp.where(strong, factor * drawn, drawn)


def level_of(rng, extent, pieces, smallest, top_value):
    loudness = 1.0
    for axis_at, shards_of in pieces:
        heights = jax.random.uniform(jax.random.fold_in(jax.random.fold_in(rng, 6), axis_at), (shards_of,), jnp.float32, smallest / len(pieces), top_value / len(pieces))
        loudness = loudness * jnp.repeat(jnp.exp(heights), extent[axis_at] // shards_of).reshape((-1,) + (1,) * (len(extent) - 1 - axis_at))
    return loudness


def centred(rng, extent, deviation, most, cuts=(), held_as=jnp.bfloat16):
    drawn = deviation * jax.random.normal(rng, extent, jnp.float32)
    if cuts:
        drawn = drawn * level_of(rng, extent, cuts, -0.22, 0.18)
    return jnp.clip(drawn, -most, most).astype(held_as)


def gaussian_with(rng, extent, deviation, limit, shards, heavy, kind=jnp.bfloat16):
    drawn = deviation * jax.random.normal(rng, extent, jnp.float32)
    if shards:
        drawn = drawn * level_of(rng, extent, shards, -0.22, 0.18)
    return jnp.clip(spiked(drawn, jax.random.fold_in(rng, 3), *heavy), -limit, limit).astype(kind)


def setup_inputs(seed: int = 0) -> dict:
    key_list = jax.random.split(jax.random.key(seed), 8)
    return {
        "tokens": gaussian_with(key_list[0], (TOKENS, D), 1.0, 6.0, ((0, 32),), (0, 1, 32, 2.75)),
        "qkv_weight": centred(key_list[1], (3 * D * D,), D ** -0.5, 0.21875, ((0, 32),)),
        "out_weight": centred(key_list[2], (D * D,), (D // 64) ** -0.5, 1.75, ((0, 32),)),
        "in_weight": centred(key_list[3], (2 * D * FF,), D ** -0.5, 0.21875, ((0, 32),)),
        "mlp_weight": centred(key_list[4], (FF * D,), (FF // 4) ** -0.5, 0.375, ((0, 32),)),
        "norm_gains": jnp.clip(1.0 + 0.1 * jax.random.normal(key_list[5], (2 * D,), jnp.float32), 0.5, 1.5).astype(jnp.bfloat16),
        "cotangent": gaussian_with(key_list[6], (TOKENS, D), 1.0, 6.0, ((0, 32),), (0, 1, 32, 2.75)),
    }


@jax.custom_vjp
def low(v):
    return lax.optimization_barrier(v.astype(jnp.bfloat16)).astype(jnp.float32)

@jax.custom_vjp
def low_back(v):
    return v

def low_keep(v):
    return (low(v), None)

def low_pass(kept, grad):
    return (grad,)

def back_keep(v):
    return (v, None)

def back_low(kept, grad):
    return (low(grad),)
low.defvjp(low_keep, low_pass)
low_back.defvjp(back_keep, back_low)

def layer_norm(values, gain):
    centered = values - lax.optimization_barrier(jnp.mean(values, axis=-1, keepdims=True))
    spread = lax.optimization_barrier(jnp.mean(centered * centered, axis=-1, keepdims=True))
    return centered * lax.rsqrt(spread + 1e-05) * gain

def rope_tables(length, head_size):
    inverse = 10000.0 ** (-jnp.arange(0, head_size, 2, dtype=jnp.float32) / head_size)
    angles = jnp.arange(length, dtype=jnp.float32)[:, None] * inverse[None, :]
    angles = jnp.concatenate([angles, angles], axis=-1)
    return (jnp.cos(angles)[:, None, :], jnp.sin(angles)[:, None, :])

def rotate(values, cosine_table, sine_table):
    midpoint = values.shape[-1] // 2
    turned = jnp.concatenate([-values[..., midpoint:], values[..., :midpoint]], axis=-1)
    return values * cosine_table + turned * sine_table

def gated_unit(joined):
    return jax.nn.gelu(joined[..., :FF], approximate=False) * joined[..., FF:]

def layer_block(group_rows, w_qkv, w_out, w_in, w_mlp, gain_attn, gain_mlp):
    highest = lax.Precision.HIGHEST
    members = group_rows.shape[0]
    normed = low(layer_norm(group_rows, gain_attn))
    projected = low_back(jnp.einsum('gtd,de->gte', normed, w_qkv, precision=highest))
    projected = projected.reshape(members, LEN, 3, HEADS, HEAD)
    cosine_table, sine_table = rope_tables(LEN, HEAD)
    queries = low(rotate(projected[:, :, 0], cosine_table, sine_table))
    key_rows = low(rotate(projected[:, :, 1], cosine_table, sine_table))
    value_rows = low(projected[:, :, 2])
    scores = low_back(jnp.einsum('gqhc,gkhc->ghqk', queries, key_rows, precision=highest) * HEAD ** (-0.5))
    places = jnp.arange(LEN)
    band_mask = jnp.abs(places[:, None] - places[None, :]) <= WIN // 2
    scores = jnp.where(band_mask, scores, -1e+30)
    attention_probs = low(jax.nn.softmax(scores, axis=-1))
    mixed_rows = jnp.einsum('ghqk,gkhc->gqhc', attention_probs, value_rows, precision=highest)
    mixed_rows = low(low_back(mixed_rows.reshape(members, LEN, D)))
    hidden = group_rows + low_back(jnp.einsum('gtd,de->gte', mixed_rows, w_out, precision=highest))
    normed_mlp = low(layer_norm(hidden, gain_mlp))
    joined = low_back(jnp.einsum('gtd,de->gte', normed_mlp, w_in, precision=highest))
    gated_rows = low(gated_unit(joined))
    return hidden + low_back(jnp.einsum('gtf,fd->gtd', gated_rows, w_mlp, precision=highest))

def reference(tokens, qkv_weight, out_weight, in_weight, mlp_weight, norm_gains, cotangent):
    sequences = TOKENS // LEN
    members = math.gcd(sequences, max(1, 4096 // LEN))

    def forward(inputs, flat_qkv, flat_out, flat_in, flat_mlp, gains):
        w_qkv = flat_qkv.reshape(D, 3 * D)
        w_out = flat_out.reshape(D, D)
        w_in = flat_in.reshape(D, 2 * FF)
        w_mlp = flat_mlp.reshape(FF, D)
        gain_attn = gains[:D]
        gain_mlp = gains[D:]

        def one_group(group_rows):
            return layer_block(group_rows, w_qkv, w_out, w_in, w_mlp, gain_attn, gain_mlp)
        groups = inputs.reshape(sequences // members, members, LEN, D)
        results = lax.map(jax.checkpoint(one_group), groups)
        return results.reshape(TOKENS, D)
    output, pullback = jax.vjp(forward, tokens.astype(jnp.float32), qkv_weight.astype(jnp.float32), out_weight.astype(jnp.float32), in_weight.astype(jnp.float32), mlp_weight.astype(jnp.float32), norm_gains.astype(jnp.float32))
    grads = pullback(cotangent.astype(jnp.float32))
    return (output.astype(jnp.bfloat16), grads[0], grads[1], grads[2], grads[3], grads[4], grads[5])
```

```python
import functools

import jax
import jax.numpy as jnp
import numpy as np
from jax import lax
from jax.experimental import pallas as pl
from jax.experimental.pallas import tpu as pltpu
from jax.sharding import PartitionSpec as P

D = 768
HEADS = 12
HEAD = 64
FF = 1152
WIN = 128
LEN = 512
PAIR = 2 * HEAD
PAIRS = HEADS // 2
BLOCK = 128
SPAN = 2 * BLOCK
BLOCKS = LEN // BLOCK
STARTS = tuple(min(max(BLOCK * i - WIN // 2, 0), LEN - SPAN) for i in range(BLOCKS))
GROUPS = ((0, 2), (2, 4))
CORE, ALONG_X, ALONG_Y, ALONG_Z = 1, 2, 4, 8
VMEM_LIMIT = 60 * 1024 * 1024
f32 = jnp.float32
bf16 = jnp.bfloat16


def dot_nn(left, right):
    return lax.dot_general(left, right, (((1,), (0,)), ((), ())), preferred_element_type=f32)


def dot_nt(left, right):
    return lax.dot_general(left, right, (((1,), (1,)), ((), ())), preferred_element_type=f32)


def dot_tn(left, right):
    return lax.dot_general(left, right, (((0,), (0,)), ((), ())), preferred_element_type=f32)


def swap(values, bits):
    return lax.ppermute(values, "fsdp", [(i, i ^ bits) for i in range(32)])


def bit_of(bits):
    return (lax.axis_index("fsdp") & bits) != 0


def ordered(bits, mine, other, axis):
    return jnp.where(
        bit_of(bits), jnp.concatenate([other, mine], axis), jnp.concatenate([mine, other], axis)
    )


def table(entries):
    return jnp.stack([jnp.stack([jnp.int32(a), jnp.int32(b)]) for a, b in entries]).astype(jnp.int32)


def split_columns(shard):
    half = shard.shape[1] // 2
    low, high = shard[:, :half], shard[:, half:]
    other = swap(jnp.where(bit_of(CORE), low, high), CORE)
    return ordered(CORE, jnp.where(bit_of(CORE), high, low), other, 0)


def gather_rows(shard, first, second):
    own = split_columns(shard)
    rows, half = own.shape
    line = jnp.stack([own] + [swap(own, ALONG_Z * j) for j in (1, 2, 3)])
    plane = jnp.concatenate([line, swap(line, first)])
    far = swap(plane, second)
    pieces = [plane, far, swap(plane, CORE), swap(far, CORE)]
    return pieces, places(rows, half, first, second, (0, 1))


def places(rows, half, first, second, sides):
    core = lax.axis_index("fsdp") & 1
    entries = []
    for side in sides:
        for beyond in (0, 1):
            for near in (0, 1):
                for j in range(4):
                    flips = (ALONG_Z * j) | (first * near) | (second * beyond)
                    chip = (lax.axis_index("fsdp") ^ flips) // 2
                    entries.append((chip * rows, (core ^ side) * half))
    return table(entries)


def gather_tall(shard):
    own = split_columns(shard)
    own = ordered(ALONG_X, own, swap(own, ALONG_X), 0)
    rows, half = own.shape
    line = jnp.stack([own] + [swap(own, ALONG_Z * j) for j in (1, 2, 3)])
    far = swap(line, ALONG_Y)
    pieces = [line, far, swap(line, CORE), swap(far, CORE)]
    return pieces, tall_places(rows, half, (0, 1))


def tall_places(rows, half, sides):
    me = lax.axis_index("fsdp")
    entries = []
    for side in sides:
        for beyond in (0, 1):
            for j in range(4):
                spot = (me ^ (ALONG_Z * j) ^ (ALONG_Y * beyond)) // 4
                entries.append((spot * rows, ((me & 1) ^ side) * half))
    return table(entries)


def gather_vector(values):
    for bits in (CORE, ALONG_X, ALONG_Y, ALONG_Z, 2 * ALONG_Z):
        values = ordered(bits, values, swap(values, bits), 0)
    return values


def scatter_vector(values):
    for bits in (2 * ALONG_Z, ALONG_Z, ALONG_Y, ALONG_X, CORE):
        half = values.shape[0] // 2
        low, high = values[:half], values[half:]
        other = swap(jnp.where(bit_of(bits), low, high), bits)
        values = jnp.where(bit_of(bits), high, low) + other
    return values


def joined_sum(kept, received):
    return (kept.astype(f32) + received.astype(f32)).astype(bf16)


def halved(kept, received):
    half = kept.shape[0] // 2
    return (
        joined_sum(kept[:half], received[:half]),
        joined_sum(kept[half:], received[half:]),
    )


def summed_line(kept, received):
    line = joined_sum(kept, received)
    total = line[0].astype(f32)
    for j in (1, 2, 3):
        total = total + swap(line[j], ALONG_Z * j).astype(f32)
    return total


def join_columns(total):
    rows = total.shape[0] // 2
    low, high = total[:rows], total[rows:]
    other = swap(jnp.where(bit_of(CORE), low, high), CORE)
    return ordered(CORE, jnp.where(bit_of(CORE), high, low), other, 1)


def scatter_rows(kept, sent, first, second):
    keep, send = halved(kept, swap(sent, CORE))
    keep, send = halved(keep, swap(send, second))
    return join_columns(summed_line(keep, swap(send, first)))


def scatter_tall(kept, sent):
    keep, send = halved(kept, swap(sent, CORE))
    total = summed_line(keep, swap(send, ALONG_Y))
    rows = total.shape[0] // 2
    low, high = total[:rows], total[rows:]
    other = swap(jnp.where(bit_of(ALONG_X), low, high).astype(bf16), ALONG_X)
    total = jnp.where(bit_of(ALONG_X), high, low) + other.astype(f32)
    return join_columns(total)


def load_pieces(places_ref, pieces, weight, sem):
    copies = []
    at = 0
    for piece in pieces:
        blocks, rows, columns = piece.shape
        for block in range(blocks):
            row = pl.multiple_of(places_ref[2 * at], 16)
            column = pl.multiple_of(places_ref[2 * at + 1], 128)
            copy = pltpu.make_async_copy(
                piece.at[block], weight.at[pl.ds(row, rows), pl.ds(column, columns)], sem
            )
            copy.start()
            copies.append(copy)
            at += 1
    return copies


def store_blocks(places_ref, total, outs):
    at = 0
    for out in outs:
        blocks, rows, columns = out.shape
        for block in range(blocks):
            row = pl.multiple_of(places_ref[2 * at], 16)
            column = pl.multiple_of(places_ref[2 * at + 1], 128)
            out[block] = total[pl.ds(row, rows), pl.ds(column, columns)].astype(bf16)
            at += 1


def turn(values, tables, sign):
    cosine, sine_up, sine_down = tables
    up = pltpu.roll(values, HEAD // 2, 1)
    down = pltpu.roll(values, PAIR - HEAD // 2, 1)
    if sign > 0:
        return values * cosine + (up * sine_up + down * sine_down)
    return values * cosine - (up * sine_up + down * sine_down)


def norm_of(values):
    centered = values - jnp.mean(values, axis=-1, keepdims=True)
    spread = jnp.mean(centered * centered, axis=-1, keepdims=True)
    scale = lax.rsqrt(spread + 1e-05)
    return centered * scale, scale


def norm_back(grad, normed, scale):
    return scale * (
        grad
        - jnp.mean(grad, axis=-1, keepdims=True)
        - normed * jnp.mean(grad * normed, axis=-1, keepdims=True)
    )


def band(block):
    key = lax.broadcasted_iota(jnp.int32, (SPAN, SPAN), 0) + STARTS[block]
    query = lax.broadcasted_iota(jnp.int32, (SPAN, SPAN), 1) % BLOCK + block * BLOCK
    return jnp.abs(key - query) <= WIN // 2


def both_heads(values, masks_ref):
    return jnp.concatenate([values * masks_ref[0:1, :], values * masks_ref[1:2, :]], axis=0)


def one_of_each(stacked):
    own = jnp.concatenate([stacked[:HEAD, :BLOCK], stacked[HEAD:, BLOCK:]], axis=0)
    return own.T


def forward_kernel(
    pairs, pieces_n, places_ref, tokens_ref, gain_ref, tables_ref, masks_ref, *refs
):
    pieces = refs[:pieces_n]
    normed_ref, qkv_ref, probs_ref, mix_ref, weight, bias, sem = refs[pieces_n:]
    first = pl.program_id(0) == 0

    @pl.when(first)
    def _():
        copies = load_pieces(places_ref, pieces, weight, sem)
        for block in range(3):
            bias[block] = jnp.where(band(block if block < 2 else BLOCKS - 1), 0.0, -1e30)
        for copy in copies:
            copy.wait()

    normed, _ = norm_of(tokens_ref[...].astype(f32))
    normed_ref[...] = (normed * gain_ref[...]).astype(bf16)
    tables = (tables_ref[0], tables_ref[1], tables_ref[2])

    def project(pair, carry):
        column = pl.multiple_of(pair * 3 * PAIR, 128)
        projected = dot_nn(normed_ref[...], weight[:, pl.ds(column, 3 * PAIR)])
        queries = turn(projected[:, :PAIR], tables, 1)
        key_rows = turn(projected[:, PAIR : 2 * PAIR], tables, 1)
        qkv_ref[:, pl.ds(column, PAIR)] = queries.astype(bf16)
        qkv_ref[:, pl.ds(column + PAIR, PAIR)] = key_rows.astype(bf16)
        qkv_ref[:, pl.ds(column + 2 * PAIR, PAIR)] = projected[:, 2 * PAIR :].astype(bf16)
        return carry

    lax.fori_loop(0, pairs, project, 0)

    def attend(pair, carry):
        column = pl.multiple_of(pair * 3 * PAIR, 128)
        out_column = pl.multiple_of(pair * PAIR, 128)
        for block in range(BLOCKS):
            rows = slice(block * BLOCK, (block + 1) * BLOCK)
            window = slice(STARTS[block], STARTS[block] + SPAN)
            queries = both_heads(qkv_ref[rows, pl.ds(column, PAIR)], masks_ref) * bf16(HEAD**-0.5)
            scores = dot_nt(qkv_ref[window, pl.ds(column + PAIR, PAIR)], queries)
            scores = scores + bias[0 if block == 0 else (2 if block == BLOCKS - 1 else 1)]
            raised = jnp.exp(scores - jnp.max(scores, axis=0, keepdims=True))
            probs = raised * (1.0 / jnp.sum(raised, axis=0, keepdims=True))
            probs = probs.astype(bf16)
            probs_ref[0, pair, block] = probs
            mixed = dot_tn(qkv_ref[window, pl.ds(column + 2 * PAIR, PAIR)], probs)
            mix_ref[rows, pl.ds(out_column, PAIR)] = one_of_each(mixed).astype(bf16)
        return carry

    lax.fori_loop(0, pairs, attend, 0)


def feed_kernel(
    groups_n,
    counts,
    *refs,
):
    refs = list(refs)
    take = lambda n: [refs.pop(0) for _ in range(n)]
    out_places, in_places, mlp_places = take(3)
    out_back, in_back, mlp_back = take(3)
    tokens_ref, cot_ref, gain_ref = take(3)
    mix_refs = take(groups_n)
    out_pieces, in_pieces, mlp_pieces = (take(n) for n in counts)
    hidden_ref, gated_ref, grad_hidden_ref = take(3)
    grad_mix_refs = take(groups_n)
    (gain_grad_ref,) = take(1)
    out_grads, in_grads, mlp_grads = (take(2 if n > 1 else 1) for n in counts)
    w_out, w_in, w_mlp, t_out, t_in, t_mlp, sems = refs
    step = pl.program_id(0)

    @pl.when(step == 0)
    def _():
        copies = load_pieces(out_places, out_pieces, w_out, sems.at[0])
        copies += load_pieces(in_places, in_pieces, w_in, sems.at[1])
        copies += load_pieces(mlp_places, mlp_pieces, w_mlp, sems.at[2])
        t_out[...] = jnp.zeros_like(t_out)
        t_in[...] = jnp.zeros_like(t_in)
        t_mlp[...] = jnp.zeros_like(t_mlp)
        gain_grad_ref[...] = jnp.zeros_like(gain_grad_ref)
        for copy in copies:
            copy.wait()

    mixed = jnp.concatenate([ref[...] for ref in mix_refs], axis=1)
    cot = cot_ref[...]
    hidden = tokens_ref[...].astype(f32) + dot_nn(mixed, w_out[...])
    hidden_ref[...] = hidden
    normed, scale = norm_of(hidden)
    gain = gain_ref[...]
    normed_mlp = (normed * gain).astype(bf16)
    grad_gated = dot_nt(cot, w_mlp[...])
    entry = dot_nn(normed_mlp, w_in[:, :FF])
    gate = dot_nn(normed_mlp, w_in[:, FF:])
    below = 0.5 * (1.0 + lax.erf(entry * 0.7071067811865476))
    density = jnp.exp(-0.5 * entry * entry) * 0.3989422804014327
    unit = entry * below
    gated = (unit * gate).astype(bf16)
    gated_ref[...] = gated
    grad_entry = ((below + entry * density) * (gate * grad_gated)).astype(bf16)
    grad_gate = (unit * grad_gated).astype(bf16)
    t_mlp[...] += dot_tn(gated, cot)
    turned = normed_mlp.T
    t_in[:, :FF] += dot_nn(turned, grad_entry)
    t_in[:, FF:] += dot_nn(turned, grad_gate)
    grad_normed = dot_nt(grad_entry, w_in[:, :FF]) + dot_nt(grad_gate, w_in[:, FF:])
    gain_grad_ref[...] += jnp.sum(grad_normed * normed, axis=0, keepdims=True)
    grad_hidden = cot.astype(f32) + norm_back(grad_normed * gain, normed, scale)
    grad_hidden_ref[...] = grad_hidden
    grad_out = grad_hidden.astype(bf16)
    t_out[...] += dot_tn(mixed, grad_out)
    column = 0
    for ref in grad_mix_refs:
        width = ref.shape[1]
        ref[...] = dot_nt(grad_out, w_out[column : column + width, :]).astype(bf16)
        column += width

    @pl.when(step == pl.num_programs(0) - 1)
    def _():
        store_blocks(out_back, t_out, out_grads)
        store_blocks(in_back, t_in, in_grads)
        store_blocks(mlp_back, t_mlp, mlp_grads)


def backward_kernel(pairs, outs_n, back_ref, normed_ref, qkv_ref, probs_ref, grad_mix_ref, tables_ref, masks_ref, *refs):
    grad_ref = refs[0]
    outs = refs[1 : 1 + outs_n]
    total, grad_keys, grad_values, grad_queries = refs[1 + outs_n :]
    step = pl.program_id(0)

    @pl.when(step == 0)
    def _():
        total[...] = jnp.zeros_like(total)

    tables = (tables_ref[0], tables_ref[1], tables_ref[2])

    def back(pair, carry):
        column = pl.multiple_of(pair * 3 * PAIR, 128)
        out_column = pl.multiple_of(pair * PAIR, 128)
        grad_keys[...] = jnp.zeros_like(grad_keys)
        grad_values[...] = jnp.zeros_like(grad_values)
        for block in range(BLOCKS):
            rows = slice(block * BLOCK, (block + 1) * BLOCK)
            window = slice(STARTS[block], STARTS[block] + SPAN)
            queries = both_heads(qkv_ref[rows, pl.ds(column, PAIR)], masks_ref) * bf16(HEAD**-0.5)
            grad_mix = both_heads(grad_mix_ref[rows, pl.ds(out_column, PAIR)], masks_ref)
            probs = probs_ref[0, pair, block]
            grad_soft = dot_nt(qkv_ref[window, pl.ds(column + 2 * PAIR, PAIR)], grad_mix)
            soft = probs.astype(f32)
            inner = jnp.sum(soft * grad_soft, axis=0, keepdims=True)
            grad_scores = (soft * (grad_soft - inner)).astype(bf16)
            grad_values[window, :] += dot_nn(probs, grad_mix)
            grad_keys[window, :] += dot_nn(grad_scores, queries)
            grad_turned = dot_tn(qkv_ref[window, pl.ds(column + PAIR, PAIR)], grad_scores)
            grad_queries[rows, :] = one_of_each(grad_turned) * HEAD**-0.5
        grad_ref[:, pl.ds(column, PAIR)] = turn(grad_queries[...], tables, -1).astype(bf16)
        grad_ref[:, pl.ds(column + PAIR, PAIR)] = turn(grad_keys[...], tables, -1).astype(bf16)
        grad_ref[:, pl.ds(column + 2 * PAIR, PAIR)] = grad_values[...].astype(bf16)
        return carry

    lax.fori_loop(0, pairs, back, 0)
    total[...] += dot_tn(normed_ref[...], grad_ref[...])

    @pl.when(step == pl.num_programs(0) - 1)
    def _():
        store_blocks(back_ref, total, outs)


def final_kernel(groups_n, counts, *refs):
    refs = list(refs)
    take = lambda n: [refs.pop(0) for _ in range(n)]
    qkv_places = take(groups_n)
    (mlp_places,) = take(1)
    tokens_ref, gain_ref, hidden_ref, gated_ref, grad_hidden_ref = take(5)
    grad_refs = take(groups_n)
    qkv_pieces = [take(n) for n in counts[:-1]]
    mlp_pieces = take(counts[-1])
    output_ref, tokens_grad_ref, gain_grad_ref = take(3)
    weights = take(groups_n)
    w_mlp, sems = refs
    step = pl.program_id(0)

    @pl.when(step == 0)
    def _():
        copies = []
        for at in range(groups_n):
            copies += load_pieces(qkv_places[at], qkv_pieces[at], weights[at], sems.at[at])
        copies += load_pieces(mlp_places, mlp_pieces, w_mlp, sems.at[groups_n])
        gain_grad_ref[...] = jnp.zeros_like(gain_grad_ref)
        for copy in copies:
            copy.wait()

    grad_normed = dot_nt(grad_refs[0][...], weights[0][...])
    for grad_ref, weight in zip(grad_refs[1:], weights[1:]):
        grad_normed = grad_normed + dot_nt(grad_ref[...], weight[...])
    normed, scale = norm_of(tokens_ref[...].astype(f32))
    gain_grad_ref[...] += jnp.sum(grad_normed * normed, axis=0, keepdims=True)
    tokens_grad_ref[...] = grad_hidden_ref[...] + norm_back(grad_normed * gain_ref[...], normed, scale)
    output_ref[...] = (hidden_ref[...] + dot_nn(gated_ref[...], w_mlp[...])).astype(bf16)


SMEM = pl.BlockSpec(memory_space=pltpu.SMEM)
ANYWHERE = pl.BlockSpec(memory_space=pl.ANY)


def rows_spec(rows, columns):
    return pl.BlockSpec((rows, columns), lambda i: (i, 0))


def whole_spec(*shape):
    return pl.BlockSpec(shape, lambda i: (0,) * len(shape))


def call(kernel, steps, inputs, outputs, scratch, flops, nbytes):
    return pl.pallas_call(
        kernel,
        grid=(steps,),
        in_specs=[spec for _, spec in inputs],
        out_specs=[spec for _, _, spec in outputs],
        out_shape=[jax.ShapeDtypeStruct(shape, dtype) for shape, dtype, _ in outputs],
        scratch_shapes=scratch,
        compiler_params=pltpu.CompilerParams(
            dimension_semantics=("arbitrary",), vmem_limit_bytes=VMEM_LIMIT
        ),
        cost_estimate=pl.CostEstimate(flops=int(flops), bytes_accessed=int(nbytes), transcendentals=0),
    )(*[array for array, _ in inputs])


def rope_constants():
    inverse = 10000.0 ** (-np.arange(0, HEAD, 2, dtype=np.float64) / HEAD)
    angles = np.arange(LEN, dtype=np.float64)[:, None] * inverse[None, :]
    angles = np.concatenate([angles] * 4, axis=-1)
    upper = (np.arange(PAIR) % HEAD >= HEAD // 2)[None, :]
    sine = np.sin(angles)
    return np.stack([np.cos(angles), np.where(upper, sine, 0.0), np.where(upper, 0.0, -sine)]).astype(
        np.float32
    )


def shards(devices, tokens, qkv_weight, out_weight, in_weight, mlp_weight, norm_gains, cotangent):
    count = tokens.shape[0]
    sequences = count // LEN
    fast = devices == 32
    orders = ((ALONG_Y, ALONG_X), (ALONG_X, ALONG_Y))

    if fast:
        gains = gather_vector(norm_gains)
        by_pair = qkv_weight.reshape(24, 3, PAIRS, PAIR).transpose(0, 2, 1, 3)
        gathered_qkv = [
            gather_rows(by_pair[:, start : start + pairs].reshape(24, pairs * 3 * PAIR), *orders[at % 2])
            for at, (start, pairs) in enumerate(GROUPS)
        ]
        gathered_in = gather_rows(in_weight.reshape(24, 2 * FF), ALONG_X, ALONG_Y)
        gathered_out = gather_rows(out_weight.reshape(24, D), ALONG_Y, ALONG_X)
        gathered_mlp = gather_tall(mlp_weight.reshape(36, D))
    else:
        whole = lambda w: lax.all_gather(w, "fsdp", axis=0, tiled=True)
        nowhere = table([(0, 0)])
        gains = whole(norm_gains)
        by_pair = whole(qkv_weight).reshape(D, 3, PAIRS, PAIR).transpose(0, 2, 1, 3)
        gathered_qkv = [
            ([by_pair[:, start : start + pairs].reshape(1, D, pairs * 3 * PAIR)], nowhere)
            for start, pairs in GROUPS
        ]
        gathered_in = ([whole(in_weight).reshape(1, D, 2 * FF)], nowhere)
        gathered_out = ([whole(out_weight).reshape(1, D, D)], nowhere)
        gathered_mlp = ([whole(mlp_weight).reshape(1, FF, D)], nowhere)
    gains = gains.astype(f32)
    gain_attn, gain_mlp = gains[:D].reshape(1, D), gains[D:].reshape(1, D)

    def back_places(rows, columns, first, second):
        if not fast:
            return table([(0, 0)]), [(1, rows, columns)]
        if first is None:
            rows, half = rows // 8, columns // 2
            return tall_places(rows, half, (0, 1)), [(8, rows, half)] * 2
        rows, half = rows // 16, columns // 2
        return places(rows, half, first, second, (0, 1)), [(16, rows, half)] * 2

    tables = jnp.asarray(rope_constants())
    masks = np.arange(PAIR)[None, :] // HEAD == np.arange(2)[:, None]
    masks = jnp.asarray(masks.astype(np.float32)).astype(bf16)
    flat = lambda spots: spots.reshape(-1)

    qkv, probs, mixes = [], [], []
    normed = None
    for at, (start, pairs) in enumerate(GROUPS):
        pieces, spots = gathered_qkv[at]
        width = pairs * 3 * PAIR
        normed, qkv_rows, group_probs, mix = call(
            functools.partial(forward_kernel, pairs, len(pieces)),
            sequences,
            [
                (flat(spots), SMEM),
                (tokens, rows_spec(LEN, D)),
                (gain_attn, whole_spec(1, D)),
                (tables, whole_spec(3, LEN, PAIR)),
                (masks, whole_spec(2, PAIR)),
            ]
            + [(piece, ANYWHERE) for piece in pieces],
            [
                ((count, D), bf16, rows_spec(LEN, D)),
                ((count, width), bf16, rows_spec(LEN, width)),
                (
                    (sequences, pairs, BLOCKS, SPAN, SPAN),
                    bf16,
                    pl.BlockSpec((1, pairs, BLOCKS, SPAN, SPAN), lambda i: (i, 0, 0, 0, 0)),
                ),
                ((count, pairs * PAIR), bf16, rows_spec(LEN, pairs * PAIR)),
            ],
            [
                pltpu.VMEM((D, width), bf16),
                pltpu.VMEM((3, SPAN, SPAN), f32),
                pltpu.SemaphoreType.DMA,
            ],
            2 * count * D * width * 2,
            count * width * 4,
        )
        qkv.append(qkv_rows)
        probs.append(group_probs)
        mixes.append(mix)

    step_rows = 256
    gathered = (gathered_out, gathered_in, gathered_mlp)
    backs = (
        back_places(D, D, ALONG_Y, ALONG_X),
        back_places(D, 2 * FF, ALONG_X, ALONG_Y),
        back_places(FF, D, None, None),
    )
    counts = tuple(len(pieces) for pieces, _ in gathered)
    grads_out = [(shape, bf16, whole_spec(*shape)) for _, shapes in backs for shape in shapes]
    results = call(
        functools.partial(feed_kernel, len(GROUPS), counts),
        count // step_rows,
        [(flat(spots), SMEM) for _, spots in gathered]
        + [(flat(spots), SMEM) for spots, _ in backs]
        + [
            (tokens, rows_spec(step_rows, D)),
            (cotangent, rows_spec(step_rows, D)),
            (gain_mlp, whole_spec(1, D)),
        ]
        + [(mix, rows_spec(step_rows, mix.shape[1])) for mix in mixes]
        + [(piece, ANYWHERE) for pieces, _ in gathered for piece in pieces],
        [
            ((count, D), f32, rows_spec(step_rows, D)),
            ((count, FF), bf16, rows_spec(step_rows, FF)),
            ((count, D), f32, rows_spec(step_rows, D)),
        ]
        + [((count, mix.shape[1]), bf16, rows_spec(step_rows, mix.shape[1])) for mix in mixes]
        + [((1, D), f32, whole_spec(1, D))]
        + grads_out,
        [
            pltpu.VMEM((D, D), bf16),
            pltpu.VMEM((D, 2 * FF), bf16),
            pltpu.VMEM((FF, D), bf16),
            pltpu.VMEM((D, D), f32),
            pltpu.VMEM((D, 2 * FF), f32),
            pltpu.VMEM((FF, D), f32),
            pltpu.SemaphoreType.DMA((3,)),
        ],
        2 * count * (3 * D * D + 6 * D * FF + 2 * D * FF),
        count * D * 16,
    )
    hidden, gated, grad_hidden = results[:3]
    grad_mixes = results[3 : 3 + len(GROUPS)]
    gain_mlp_grad = results[3 + len(GROUPS)]
    weight_grads = results[4 + len(GROUPS) :]

    def scatter(blocks, first, second):
        if not fast:
            return lax.psum_scatter(
                blocks[0].astype(f32).reshape(-1), "fsdp", scatter_dimension=0, tiled=True
            )
        if first is None:
            return scatter_tall(*blocks).reshape(-1)
        return scatter_rows(*blocks, first, second).reshape(-1)

    each = 2 if fast else 1
    mlp_share = scatter(weight_grads[2 * each :], None, None)
    in_share = scatter(weight_grads[each : 2 * each], ALONG_X, ALONG_Y)
    out_share = scatter(weight_grads[:each], ALONG_Y, ALONG_X)

    grads = [None] * len(GROUPS)
    qkv_shares = [None] * len(GROUPS)
    for at in reversed(range(len(GROUPS))):
        start, pairs = GROUPS[at]
        width = pairs * 3 * PAIR
        spots, shapes = back_places(D, width, *orders[at % 2])
        results = call(
            functools.partial(backward_kernel, pairs, len(shapes)),
            sequences,
            [
                (flat(spots), SMEM),
                (normed, rows_spec(LEN, D)),
                (qkv[at], rows_spec(LEN, width)),
                (
                    probs[at],
                    pl.BlockSpec((1, pairs, BLOCKS, SPAN, SPAN), lambda i: (i, 0, 0, 0, 0)),
                ),
                (grad_mixes[at], rows_spec(LEN, pairs * PAIR)),
                (tables, whole_spec(3, LEN, PAIR)),
                (masks, whole_spec(2, PAIR)),
            ],
            [((count, width), bf16, rows_spec(LEN, width))]
            + [(shape, bf16, whole_spec(*shape)) for shape in shapes],
            [
                pltpu.VMEM((D, width), f32),
                pltpu.VMEM((LEN, PAIR), f32),
                pltpu.VMEM((LEN, PAIR), f32),
                pltpu.VMEM((LEN, PAIR), f32),
            ],
            2 * count * D * width * 2,
            count * width * 4,
        )
        grads[at] = results[0]
        qkv_shares[at] = scatter(results[1:], *orders[at % 2]) if fast else results[1:]

    if fast:
        qkv_share = jnp.concatenate(
            [share.reshape(24, pairs, 3, PAIR) for share, (_, pairs) in zip(qkv_shares, GROUPS)], axis=1
        )
        qkv_share = qkv_share.transpose(0, 2, 1, 3).reshape(-1)
    else:
        qkv_share = jnp.concatenate(
            [blocks[0].reshape(D, pairs, 3, PAIR) for blocks, (_, pairs) in zip(qkv_shares, GROUPS)], axis=1
        )
        qkv_share = scatter([qkv_share.transpose(0, 2, 1, 3)], None, None)

    counts = tuple(len(pieces) for pieces, _ in gathered_qkv) + (len(gathered_mlp[0]),)
    output, tokens_grad, gain_attn_grad = call(
        functools.partial(final_kernel, len(GROUPS), counts),
        count // step_rows,
        [(flat(spots), SMEM) for _, spots in gathered_qkv]
        + [(flat(gathered_mlp[1]), SMEM)]
        + [
            (tokens, rows_spec(step_rows, D)),
            (gain_attn, whole_spec(1, D)),
            (hidden, rows_spec(step_rows, D)),
            (gated, rows_spec(step_rows, FF)),
            (grad_hidden, rows_spec(step_rows, D)),
        ]
        + [(grad, rows_spec(step_rows, grad.shape[1])) for grad in grads]
        + [(piece, ANYWHERE) for pieces, _ in gathered_qkv for piece in pieces]
        + [(piece, ANYWHERE) for piece in gathered_mlp[0]],
        [
            ((count, D), bf16, rows_spec(step_rows, D)),
            ((count, D), f32, rows_spec(step_rows, D)),
            ((1, D), f32, whole_spec(1, D)),
        ],
        [pltpu.VMEM((D, pairs * 3 * PAIR), bf16) for _, pairs in GROUPS]
        + [pltpu.VMEM((FF, D), bf16), pltpu.SemaphoreType.DMA((len(GROUPS) + 1,))],
        2 * count * (3 * D * D + FF * D),
        count * D * 20,
    )
    gains_grad = jnp.concatenate([gain_attn_grad.reshape(-1), gain_mlp_grad.reshape(-1)])
    if fast:
        gains_share = scatter_vector(gains_grad)
    else:
        gains_share = lax.psum_scatter(gains_grad, "fsdp", scatter_dimension=0, tiled=True)
    return (output, tokens_grad, qkv_share, out_share, in_share, mlp_share, gains_share)


def solution(mesh):
    placed = (P("fsdp", None),) + (P("fsdp"),) * 5 + (P("fsdp", None),)
    return jax.shard_map(
        functools.partial(shards, mesh.shape["fsdp"]),
        mesh=mesh,
        in_specs=placed,
        out_specs=(P("fsdp", None),) * 2 + (P("fsdp"),) * 5,
        check_vma=False,
    )
```

```python
import functools

import jax
import jax.numpy as jnp
import numpy as np
from jax import lax
from jax.experimental import pallas as pl
from jax.experimental.pallas import tpu as pltpu
from jax.sharding import PartitionSpec as P

D = 768
HEADS = 12
HEAD = 64
FF = 1152
WIN = 128
LEN = 512
PAIR = 2 * HEAD
PAIRS = HEADS // 2
BLOCK = 128
SPAN = 2 * BLOCK
BLOCKS = LEN // BLOCK
STARTS = tuple(min(max(BLOCK * i - WIN // 2, 0), LEN - SPAN) for i in range(BLOCKS))
GROUPS = 3
EACH = PAIRS // GROUPS
WIDTH = EACH * 3 * PAIR
CORE, ALONG_X, ALONG_Y, ALONG_Z = 1, 2, 4, 8
NOWHERE = (0, 0, 0, 0, 0, 0, 0)
VMEM_LIMIT = 60 * 1024 * 1024
f32 = jnp.float32
bf16 = jnp.bfloat16


def dot_nn(left, right):
    return lax.dot_general(left, right, (((1,), (0,)), ((), ())), preferred_element_type=f32)


def dot_nt(left, right):
    return lax.dot_general(left, right, (((1,), (1,)), ((), ())), preferred_element_type=f32)


def dot_tn(left, right):
    return lax.dot_general(left, right, (((0,), (0,)), ((), ())), preferred_element_type=f32)


def swap(values, bits):
    return lax.ppermute(values, "fsdp", [(i, i ^ bits) for i in range(32)])


def bit_of(bits):
    return (lax.axis_index("fsdp") & bits) != 0


def ordered(bits, mine, other, axis):
    return jnp.where(
        bit_of(bits), jnp.concatenate([other, mine], axis), jnp.concatenate([mine, other], axis)
    )


def after(values, token):
    return jnp.where(token[(0,) * token.ndim].astype(f32) < jnp.inf, values, jnp.zeros_like(values))


def split_columns(shard):
    half = shard.shape[1] // 2
    low, high = shard[:, :half], shard[:, half:]
    other = swap(jnp.where(bit_of(CORE), low, high), CORE)
    return ordered(CORE, jnp.where(bit_of(CORE), high, low), other, 0)


def along_line(own):
    return jnp.stack([own] + [swap(own, ALONG_Z * j) for j in (1, 2, 3)])


def chip_flips(count, first, second):
    return [ALONG_Z * (at % 4) | first * (at // 4 % 2) | second * (at // 8) for at in range(count)]


def swap_half(values, bits):
    half = values.shape[0] // 2
    low, high = values[:half], values[half:]
    other = swap(jnp.where(bit_of(bits), low, high), bits)
    return jnp.where(bit_of(bits), high, low), other


def joined_sum(kept, received):
    return (kept.astype(f32) + received.astype(f32)).astype(bf16)


def halved(kept, received):
    half = kept.shape[0] // 2
    return (
        joined_sum(kept[:half], received[:half]),
        joined_sum(kept[half:], received[half:]),
    )


def summed_line(line):
    total = line[0].astype(f32)
    for j in (1, 2, 3):
        total = total + swap(line[j], ALONG_Z * j).astype(f32)
    return total


def join_columns(total):
    rows = total.shape[0] // 2
    low, high = total[:rows], total[rows:]
    other = swap(jnp.where(bit_of(CORE), low, high), CORE)
    return jnp.where(bit_of(CORE), high, low), other


def both_columns(joined, start, stop):
    mine, other = joined
    return ordered(CORE, mine[:, start:stop], other[:, start:stop], 1)


def place(me_ref, spot):
    flips, shift, rows, row, side, columns, column = spot
    me = me_ref[0]
    return (
        pl.multiple_of(((me ^ flips) >> shift) * rows + row, 16),
        pl.multiple_of(((me & 1) ^ side) * columns + column, 128),
    )


def load_pieces(me_ref, loads, spots, arrays, weights, sem):
    copies = []
    for at, (array, block, start, width, weight) in enumerate(loads):
        piece = arrays[array].at[block, :, pl.ds(start, width)]
        rows = arrays[array].shape[1]
        row, column = place(me_ref, spots[at])
        copy = pltpu.make_async_copy(piece, weights[weight].at[pl.ds(row, rows), pl.ds(column, width)], sem)
        copy.start()
        copies.append(copy)
    return copies


def store_blocks(me_ref, spots, total, outs):
    at = 0
    for out in outs:
        blocks, rows, columns = out.shape
        for block in range(blocks):
            row, column = place(me_ref, spots[at])
            out[block] = total[pl.ds(row, rows), pl.ds(column, columns)].astype(bf16)
            at += 1


def turn(values, tables, sign):
    cosine, sine_up, sine_down = tables
    up = pltpu.roll(values, HEAD // 2, 1)
    down = pltpu.roll(values, PAIR - HEAD // 2, 1)
    if sign > 0:
        return values * cosine + (up * sine_up + down * sine_down)
    return values * cosine - (up * sine_up + down * sine_down)


def norm_of(values):
    centered = values - jnp.mean(values, axis=-1, keepdims=True)
    spread = jnp.mean(centered * centered, axis=-1, keepdims=True)
    scale = lax.rsqrt(spread + 1e-05)
    return centered * scale, scale


def norm_back(grad, normed, scale):
    return scale * (
        grad
        - jnp.mean(grad, axis=-1, keepdims=True)
        - normed * jnp.mean(grad * normed, axis=-1, keepdims=True)
    )


def band(block):
    key = lax.broadcasted_iota(jnp.int32, (SPAN, SPAN), 0) + STARTS[block]
    query = lax.broadcasted_iota(jnp.int32, (SPAN, SPAN), 1) % BLOCK + block * BLOCK
    return jnp.abs(key - query) <= WIN // 2


def both_heads(values, masks_ref):
    return jnp.concatenate([values * masks_ref[0:1, :], values * masks_ref[1:2, :]], axis=0)


def apart(turned):
    nothing = jnp.zeros((HEAD, turned.shape[1]), turned.dtype)
    first = jnp.concatenate([turned[:HEAD], nothing], axis=0)
    second = jnp.concatenate([nothing, turned[HEAD:]], axis=0)
    return jnp.concatenate([first, second], axis=1)


def one_of_each(stacked):
    return jnp.concatenate([stacked[:HEAD, :BLOCK], stacked[HEAD:, BLOCK:]], axis=0)


def turned_windows(values):
    straight = values.T
    shifted = values[STARTS[1] : LEN - STARTS[1]].T
    return [
        straight[:, :SPAN],
        shifted[:, :SPAN],
        shifted[:, BLOCK : BLOCK + SPAN],
        straight[:, LEN - SPAN :],
    ]


def staggered(tiles, first, second, third):
    ones, twos = {}, {}
    for at in range(len(tiles) + 2):
        if at < len(tiles):
            ones[at] = first(*tiles[at])
        if 1 <= at <= len(tiles):
            twos[at - 1] = second(*tiles[at - 1], ones.pop(at - 1))
        if at >= 2:
            third(*tiles[at - 2], twos.pop(at - 2))


def forward_kernel(loads, spots, arrays_n, me_ref, rows_ref, gain_ref, tables_ref, masks_ref, *refs):
    arrays = refs[:arrays_n]
    qkv_ref, probs_ref, mix_ref, *normed_ref, weight, bias, sem = refs[arrays_n:]

    @pl.when(pl.program_id(0) == 0)
    def _():
        copies = load_pieces(me_ref, loads, spots, arrays, [weight], sem)
        for block in range(3):
            bias[block] = jnp.where(band(block if block < 2 else BLOCKS - 1), 0.0, -1e30)
        for copy in copies:
            copy.wait()

    if normed_ref:
        normed, _ = norm_of(rows_ref[...].astype(f32))
        normed_ref[0][...] = (normed * gain_ref[...]).astype(bf16)
        rows_ref = normed_ref[0]
    tables = (tables_ref[0], tables_ref[1], tables_ref[2])

    projected = dot_nn(rows_ref[...], weight[...])
    for pair in range(EACH):
        column = pair * 3 * PAIR
        queries = turn(projected[:, column : column + PAIR], tables, 1)
        key_rows = turn(projected[:, column + PAIR : column + 2 * PAIR], tables, 1)
        qkv_ref[:, column : column + PAIR] = queries.astype(bf16) * bf16(HEAD**-0.5)
        qkv_ref[:, column + PAIR : column + 2 * PAIR] = key_rows.astype(bf16)
        qkv_ref[:, column + 2 * PAIR : column + 3 * PAIR] = projected[
            :, column + 2 * PAIR : column + 3 * PAIR
        ].astype(bf16)

    turned_queries, values = [], []
    for pair in range(EACH):
        column = pair * 3 * PAIR
        turned_queries.append(qkv_ref[:, column : column + PAIR].T)
        values.append(turned_windows(qkv_ref[:, column + 2 * PAIR : column + 3 * PAIR]))
    mixed = [[None] * BLOCKS for _ in range(EACH)]

    def score(pair, block):
        key_column = pair * 3 * PAIR + PAIR
        rows = slice(block * BLOCK, (block + 1) * BLOCK)
        window = slice(STARTS[block], STARTS[block] + SPAN)
        return dot_nn(qkv_ref[window, key_column : key_column + PAIR], apart(turned_queries[pair][:, rows]))

    def weigh(pair, block, scores):
        scores = scores + bias[0 if block == 0 else (2 if block == BLOCKS - 1 else 1)]
        raised = jnp.exp(scores - jnp.max(scores, axis=0, keepdims=True))
        probs = (raised * (1.0 / jnp.sum(raised, axis=0, keepdims=True))).astype(bf16)
        probs_ref[0, 0, pair, block] = probs
        return probs

    def mix(pair, block, probs):
        mixed[pair][block] = one_of_each(dot_nn(values[pair][block], probs)).astype(bf16)
        if block == BLOCKS - 1:
            mix_ref[:, pair * PAIR : (pair + 1) * PAIR] = jnp.concatenate(mixed[pair], axis=1).T

    staggered([(pair, block) for pair in range(EACH) for block in range(BLOCKS)], score, weigh, mix)


def feed_kernel(loads, spots, arrays_n, backs, *refs):
    refs = list(refs)
    take = lambda n: [refs.pop(0) for _ in range(n)]
    (me_ref,) = take(1)
    tokens_ref, cot_ref, gain_ref = take(3)
    (mix_ref,) = take(1)
    arrays = take(arrays_n)
    hidden_ref, gated_ref, grad_hidden_ref = take(3)
    (grad_mix_ref,) = take(1)
    (gain_grad_ref,) = take(1)
    out_grads, in_grads, mlp_grads = (take(len(back[1])) for back in backs)
    w_out, w_in, w_mlp, t_out, t_in, t_mlp, sem = refs
    step = pl.program_id(0)

    @pl.when(step == 0)
    def _():
        copies = load_pieces(me_ref, loads, spots, arrays, [w_out, w_in, w_mlp], sem)
        t_out[...] = jnp.zeros_like(t_out)
        t_in[...] = jnp.zeros_like(t_in)
        t_mlp[...] = jnp.zeros_like(t_mlp)
        gain_grad_ref[...] = jnp.zeros_like(gain_grad_ref)
        for copy in copies:
            copy.wait()

    mixed = mix_ref[...]
    cot = cot_ref[...]
    hidden = tokens_ref[...].astype(f32) + dot_nn(mixed, w_out[...])
    hidden_ref[...] = hidden
    normed, scale = norm_of(hidden)
    gain = gain_ref[...]
    normed_mlp = (normed * gain).astype(bf16)
    grad_gated = dot_nt(cot, w_mlp[...])
    entry = dot_nn(normed_mlp, w_in[:, :FF])
    gate = dot_nn(normed_mlp, w_in[:, FF:])
    below = 0.5 * (1.0 + lax.erf(entry * 0.7071067811865476))
    density = jnp.exp(-0.5 * entry * entry) * 0.3989422804014327
    unit = entry * below
    gated = (unit * gate).astype(bf16)
    gated_ref[...] = gated
    grad_entry = ((below + entry * density) * (gate * grad_gated)).astype(bf16)
    grad_gate = (unit * grad_gated).astype(bf16)
    t_mlp[...] += dot_tn(gated, cot)
    turned = normed_mlp.T
    t_in[:, :FF] += dot_nn(turned, grad_entry)
    t_in[:, FF:] += dot_nn(turned, grad_gate)
    grad_normed = dot_nt(grad_entry, w_in[:, :FF]) + dot_nt(grad_gate, w_in[:, FF:])
    gain_grad_ref[...] += jnp.sum(grad_normed * normed, axis=0, keepdims=True)
    grad_hidden = cot.astype(f32) + norm_back(grad_normed * gain, normed, scale)
    grad_hidden_ref[...] = grad_hidden
    grad_out = grad_hidden.astype(bf16)
    t_out[...] += dot_tn(mixed, grad_out)
    grad_mix_ref[...] = dot_nt(grad_out, w_out[...]).astype(bf16)

    @pl.when(step == pl.num_programs(0) - 1)
    def _():
        store_blocks(me_ref, backs[0][0], t_out, out_grads)
        store_blocks(me_ref, backs[1][0], t_in, in_grads)
        store_blocks(me_ref, backs[2][0], t_mlp, mlp_grads)


def backward_kernel(
    spots, outs_n, me_ref, normed_ref, qkv_ref, probs_ref, grad_mix_ref, tables_ref, masks_ref, *refs
):
    grad_ref = refs[0]
    outs = refs[1 : 1 + outs_n]
    total, grad_keys, grad_values = refs[1 + outs_n :]
    step = pl.program_id(0)

    @pl.when(step == 0)
    def _():
        total[...] = jnp.zeros_like(total)

    tables = (tables_ref[0], tables_ref[1], tables_ref[2])

    grad_keys[...] = jnp.zeros_like(grad_keys)
    grad_values[...] = jnp.zeros_like(grad_values)
    turned_grads, turned_keys = [], []
    for pair in range(EACH):
        column = pair * 3 * PAIR + PAIR
        turned_grads.append(grad_mix_ref[:, pair * PAIR : (pair + 1) * PAIR].T)
        turned_keys.append(turned_windows(qkv_ref[:, column : column + PAIR]))
    grad_queries = [[None] * BLOCKS for _ in range(EACH)]

    def soften(pair, block):
        column = pair * 3 * PAIR + 2 * PAIR
        rows = slice(block * BLOCK, (block + 1) * BLOCK)
        window = slice(STARTS[block], STARTS[block] + SPAN)
        return dot_nn(qkv_ref[window, column : column + PAIR], apart(turned_grads[pair][:, rows]))

    def score(pair, block, grad_soft):
        soft = probs_ref[0, 0, pair, block].astype(f32)
        inner = jnp.sum(soft * grad_soft, axis=0, keepdims=True)
        return (soft * (grad_soft - inner)).astype(bf16)

    def spread(pair, block, grad_scores):
        column = pair * 3 * PAIR
        own = slice(pair * PAIR, (pair + 1) * PAIR)
        rows = slice(block * BLOCK, (block + 1) * BLOCK)
        window = slice(STARTS[block], STARTS[block] + SPAN)
        queries = both_heads(qkv_ref[rows, column : column + PAIR], masks_ref)
        grad_mix = both_heads(grad_mix_ref[rows, own], masks_ref)
        grad_values[window, own] += dot_nn(probs_ref[0, 0, pair, block], grad_mix)
        grad_keys[window, own] += dot_nn(grad_scores, queries)
        grad_queries[pair][block] = one_of_each(dot_nn(turned_keys[pair][block], grad_scores))
        if block == BLOCKS - 1:
            turned = jnp.concatenate(grad_queries[pair], axis=1).T * HEAD**-0.5
            grad_ref[:, column : column + PAIR] = turn(turned, tables, -1).astype(bf16)
            grad_ref[:, column + PAIR : column + 2 * PAIR] = turn(grad_keys[:, own], tables, -1).astype(bf16)
            grad_ref[:, column + 2 * PAIR : column + 3 * PAIR] = grad_values[:, own].astype(bf16)

    staggered([(pair, block) for pair in range(EACH) for block in range(BLOCKS)], soften, score, spread)
    total[...] += dot_tn(normed_ref[...], grad_ref[...])

    @pl.when(step == pl.num_programs(0) - 1)
    def _():
        store_blocks(me_ref, spots, total, outs)


def final_kernel(loads, spots, arrays_n, me_ref, tokens_ref, gain_ref, grad_hidden_ref, grad_ref, *refs):
    arrays = refs[:arrays_n]
    tokens_grad_ref, gain_grad_ref, weight, sem = refs[arrays_n:]

    @pl.when(pl.program_id(0) == 0)
    def _():
        copies = load_pieces(me_ref, loads, spots, arrays, [weight], sem)
        gain_grad_ref[...] = jnp.zeros_like(gain_grad_ref)
        for copy in copies:
            copy.wait()

    grad_normed = dot_nt(grad_ref[...], weight[...])
    normed, scale = norm_of(tokens_ref[...].astype(f32))
    gain_grad_ref[...] += jnp.sum(grad_normed * normed, axis=0, keepdims=True)
    tokens_grad_ref[...] = grad_hidden_ref[...] + norm_back(grad_normed * gain_ref[...], normed, scale)


def output_kernel(loads, spots, arrays_n, me_ref, hidden_ref, gated_ref, *refs):
    arrays = refs[:arrays_n]
    output_ref, weight, sem = refs[-3:]

    @pl.when(pl.program_id(0) == 0)
    def _():
        for copy in load_pieces(me_ref, loads, spots, arrays, [weight], sem):
            copy.wait()

    output_ref[...] = (hidden_ref[...] + dot_nn(gated_ref[...], weight[...])).astype(bf16)


SMEM = pl.BlockSpec(memory_space=pltpu.SMEM)
ANYWHERE = pl.BlockSpec(memory_space=pl.ANY)


def rows_spec(rows, columns):
    return pl.BlockSpec((rows, columns), lambda i: (i, 0))


def whole_spec(*shape):
    return pl.BlockSpec(shape, lambda i: (0,) * len(shape))


def call(kernel, steps, inputs, outputs, scratch, flops, nbytes, waits=(), through=(), into=()):
    extra = list(waits) + list(through) + list(into)
    n_in, n_out, n_through = len(inputs), len(outputs), len(through)
    begin = n_in + len(extra)

    def trimmed(*refs):
        kernel(*refs[:n_in], *refs[begin : begin + n_out], *refs[begin + n_out + n_through :])

    aliases = {n_in + len(waits) + at: n_out + at for at in range(n_through)}
    aliases.update({n_in + len(waits) + n_through + at: at for at in range(len(into))})
    results = pl.pallas_call(
        trimmed,
        grid=(steps,),
        in_specs=[spec for _, spec in inputs] + [ANYWHERE] * len(extra),
        out_specs=[spec for _, _, spec in outputs] + [ANYWHERE] * n_through,
        out_shape=[jax.ShapeDtypeStruct(shape, dtype) for shape, dtype, _ in outputs]
        + [jax.ShapeDtypeStruct(array.shape, array.dtype) for array in through],
        scratch_shapes=scratch,
        input_output_aliases=aliases,
        compiler_params=pltpu.CompilerParams(
            dimension_semantics=("arbitrary",), vmem_limit_bytes=VMEM_LIMIT
        ),
        cost_estimate=pl.CostEstimate(flops=int(flops), bytes_accessed=int(nbytes), transcendentals=0),
    )(*[array for array, _ in inputs], *extra)
    if not through:
        return results
    return results[:n_out], results[n_out:]


def rope_constants():
    inverse = 10000.0 ** (-np.arange(0, HEAD, 2, dtype=np.float64) / HEAD)
    angles = np.arange(LEN, dtype=np.float64)[:, None] * inverse[None, :]
    angles = np.concatenate([angles] * 4, axis=-1)
    upper = (np.arange(PAIR) % HEAD >= HEAD // 2)[None, :]
    sine = np.sin(angles)
    return np.stack([np.cos(angles), np.where(upper, sine, 0.0), np.where(upper, 0.0, -sine)]).astype(
        np.float32
    )


def spread_loads(arrays, flips, start, width, weight, column):
    loads, spots = [], []
    for index, blocks, first_chip, other in arrays:
        for block in range(blocks):
            loads.append((index, block, start, width, weight))
            spots.append((flips[first_chip + block], 1, 48, 0, other, width, column))
    return loads, spots


def gather_weights(qkv_weight, out_weight, in_weight, mlp_weight, norm_gains):
    by_pair = qkv_weight.reshape(24, 3, PAIRS, PAIR).transpose(0, 2, 1, 3).reshape(24, PAIRS, 3 * PAIR)
    gain_row = jnp.pad(norm_gains.reshape(1, 48), ((0, 23), (0, 80)))
    early = split_columns(
        jnp.concatenate([by_pair[:, 0], gain_row, by_pair[:, 1], gain_row], axis=1)
    )
    later = split_columns(
        jnp.concatenate([by_pair[:, 2], by_pair[:, 4], by_pair[:, 3], by_pair[:, 5]], axis=1)
    )
    own_in = split_columns(in_weight.reshape(24, 2 * FF))
    own_out = split_columns(out_weight.reshape(24, D))
    own_mlp = split_columns(mlp_weight.reshape(36, D))
    own_mlp = ordered(ALONG_X, own_mlp, swap(own_mlp, ALONG_X), 0)

    line = along_line(early)
    plane = jnp.concatenate([line, swap(line, ALONG_X)])
    far = swap(plane, ALONG_Y)
    first_arrays = [plane, far, swap(plane, CORE), swap(far, CORE)]
    chips = chip_flips(16, ALONG_X, ALONG_Y)
    slots = [(0, 8, 0, 0), (1, 8, 8, 0), (2, 8, 0, 1), (3, 8, 8, 1)]
    first = (first_arrays, *spread_loads(slots, chips, 0, 3 * PAIR, 0, 0))
    scales = jnp.concatenate([plane, far])[:, :, 3 * PAIR : 3 * PAIR + 48]
    scales = jnp.concatenate([scales[:, 0], scales[:, 24]], axis=1)
    held = (lax.axis_index("fsdp") ^ np.asarray(chips, np.int32)) // 2
    spot = held[None, :] == np.arange(16, dtype=np.int32)[:, None]
    gains = dot_nn(spot.astype(bf16), scales).reshape(-1)

    line = along_line(after(later, line))
    early_plane = plane
    plane = jnp.concatenate([line, swap(line, ALONG_Y)])
    far = swap(plane, ALONG_X)
    other_arrays = [plane, far, swap(plane, CORE), swap(far, CORE)]
    chips = chip_flips(16, ALONG_Y, ALONG_X)
    others = [
        (other_arrays, *spread_loads(slots, chips, 3 * PAIR * at, 3 * PAIR, 0, 0)) for at in range(2)
    ]

    rows = own_mlp.shape[0] // 3
    thirds = [own_mlp[rows * i : rows * (i + 1)] for i in range(3)]
    own = after(jnp.concatenate([own_in, own_out] + thirds, axis=1), early_plane)
    start_out, start_mlp = FF, FF + D // 2
    parts = [own] + [swap(own, ALONG_Z * j) for j in (1, 2, 3)]
    rest_arrays = []

    def near(own_mlp):
        thirds = [own_mlp[rows * i : rows * (i + 1)] for i in range(3)]
        own = jnp.concatenate([own_in, own_out] + thirds, axis=1)
        line = jnp.stack([own] + parts[1:])
        return line, line[:, :, :start_mlp], swap(line, ALONG_Y)

    def far(line, head, beside):
        mlp = jnp.concatenate([line[:, :, start_mlp:], beside[:, :, start_mlp:]])
        other_head = beside[:, :, :start_mlp]
        return other_head, swap(jnp.concatenate([head, other_head]), ALONG_X), mlp, swap(mlp, CORE)

    def across(head, other_head, beyond, mlp, mlp_other):
        both = jnp.concatenate([head, other_head, beyond])
        rest_arrays.extend([both, swap(both, CORE), mlp, mlp_other])

    chips = chip_flips(16, ALONG_Y, ALONG_X)
    rest_slots = [(0, 16, 0, 0), (1, 16, 0, 1)]
    in_loads, in_spots = spread_loads(rest_slots, chips, 0, FF, 1, 0)
    out_loads, out_spots = spread_loads(rest_slots, chips, start_out, D // 2, 0, 0)
    mlp_loads, mlp_spots = [], []
    for other in (0, 1):
        for block, flips in enumerate(chip_flips(8, ALONG_Y, 0)):
            for third in range(3):
                mlp_loads.append((2 + other, block, third * (D // 2), D // 2, 2))
                mlp_spots.append((flips, 2, 144, third * 48, other, D // 2, 0))
    rest = (rest_arrays, out_loads + in_loads + mlp_loads, out_spots + in_spots + mlp_spots)

    last_loads, last_spots = list(first[1]), list(first[2])
    for group in range(2):
        column = WIDTH * (group + 1)
        more = spread_loads(slots, chips, 3 * PAIR * group, 3 * PAIR, 0, column)
        last_loads += [(load[0] + 4,) + load[1:] for load in more[0]]
        last_spots += more[1]
    end_loads = [(load[0] - 2,) + load[1:4] + (0,) for load in mlp_loads]
    last = lambda: (first_arrays + other_arrays, last_loads, last_spots)
    ends = lambda: (rest_arrays[2:], end_loads, mlp_spots)
    return gains, [first] + others, rest, last, ends, (own_mlp, parts[1:], near, far, across)


def gather_simply(qkv_weight, out_weight, in_weight, mlp_weight, norm_gains):
    whole = lambda w: lax.all_gather(w, "fsdp", axis=0, tiled=True)
    by_pair = whole(qkv_weight).reshape(D, 3, PAIRS, PAIR).transpose(0, 2, 1, 3)
    w_qkv = by_pair.reshape(1, D, 3 * D)
    w_in, w_out = whole(in_weight).reshape(1, D, 2 * FF), whole(out_weight).reshape(1, D, D)
    w_mlp = whole(mlp_weight).reshape(1, FF, D)
    groups = [([w_qkv], [(0, 0, at * WIDTH, WIDTH, 0)], [NOWHERE]) for at in range(GROUPS)]
    rest = (
        [w_out, w_in, w_mlp],
        [(0, 0, 0, D, 0), (1, 0, 0, 2 * FF, 1), (2, 0, 0, D, 2)],
        [NOWHERE] * 3,
    )
    last = lambda: ([w_qkv], [(0, 0, 0, 3 * D, 0)], [NOWHERE])
    ends = lambda: ([w_mlp], [(0, 0, 0, D, 0)], [NOWHERE])
    return whole(norm_gains), groups, rest, last, ends, None


def shards(devices, tokens, qkv_weight, out_weight, in_weight, mlp_weight, norm_gains, cotangent):
    count = tokens.shape[0]
    sequences = count // LEN
    fast = devices == 32
    gather = gather_weights if fast else gather_simply
    gains, groups, rest, last, ends, rounds = gather(
        qkv_weight, out_weight, in_weight, mlp_weight, norm_gains
    )
    gains = gains.astype(f32)
    gain_attn, gain_mlp = gains[:D].reshape(1, D), gains[D:].reshape(1, D)
    me = lax.axis_index("fsdp").astype(jnp.int32).reshape(1)

    def back_places(rows, columns, first, second):
        if not fast:
            return [NOWHERE], [(1, rows, columns)]
        half = columns // 2
        blocks = 8 if second is None else 16
        rows = rows // blocks
        spots = [
            (flips, 2 if second is None else 1, rows, 0, other, half, 0)
            for other in (0, 1)
            for flips in chip_flips(blocks, first, second or 0)
        ]
        return spots, [(blocks, rows, half)] * 2

    tables = jnp.asarray(rope_constants())
    masks = np.arange(PAIR)[None, :] // HEAD == np.arange(2)[:, None]
    masks = jnp.asarray(masks.astype(np.float32)).astype(bf16)
    probs_shape = (GROUPS, sequences, EACH, BLOCKS, SPAN, SPAN)
    probs_spec = lambda at: pl.BlockSpec((1, 1) + probs_shape[2:], lambda i: (at, i, 0, 0, 0, 0))
    group_spec = lambda at, columns: pl.BlockSpec((LEN, columns), lambda i: (i, at))

    kept = []

    def forward(at, waits, through):
        arrays, loads, spots = groups[at]
        outputs = [
            ((count, 3 * D), bf16, group_spec(at, WIDTH)),
            (probs_shape, bf16, probs_spec(at)),
            ((count, D), bf16, group_spec(at, EACH * PAIR)),
        ]
        if at == 0:
            outputs.append(((count, D), bf16, rows_spec(LEN, D)))
        results = call(
            functools.partial(forward_kernel, loads, spots, len(arrays)),
            sequences,
            [
                (me, SMEM),
                (kept[3] if kept else tokens, rows_spec(LEN, D)),
                (gain_attn, whole_spec(1, D)),
                (tables, whole_spec(3, LEN, PAIR)),
                (masks, whole_spec(2, PAIR)),
            ]
            + [(array, ANYWHERE) for array in arrays],
            outputs,
            [
                pltpu.VMEM((D, WIDTH), bf16),
                pltpu.VMEM((3, SPAN, SPAN), f32),
                pltpu.SemaphoreType.DMA,
            ],
            4 * count * D * WIDTH,
            count * WIDTH * 8,
            waits=waits,
            through=through,
            into=kept[:3],
        )
        results, handed = results if through else (results, [])
        kept[: len(results)] = results
        return handed

    if fast:
        own_mlp, parts, near, far, across = rounds
        (own_mlp,) = forward(0, [], [own_mlp])
        line, head, beside = near(own_mlp)
        (head,) = forward(1, parts, [head])
        other_head, beyond, mlp, mlp_other = far(line, head, beside)
        (head,) = forward(2, [], [head])
        across(head, other_head, beyond, mlp, mlp_other)
    else:
        for at in range(GROUPS):
            forward(at, [], [])
    qkv, probs, mix, normed = kept

    step_rows = 256
    arrays, loads, spots = rest
    backs = (
        back_places(D, D, ALONG_X, ALONG_Y),
        back_places(D, 2 * FF, ALONG_Y, ALONG_X),
        back_places(FF, D, ALONG_Y, None),
    )
    results = call(
        functools.partial(feed_kernel, loads, spots, len(arrays), backs),
        count // step_rows,
        [(me, SMEM)]
        + [
            (tokens, rows_spec(step_rows, D)),
            (cotangent, rows_spec(step_rows, D)),
            (gain_mlp, whole_spec(1, D)),
        ]
        + [(mix, rows_spec(step_rows, D))]
        + [(array, ANYWHERE) for array in arrays],
        [
            ((count, D), f32, rows_spec(step_rows, D)),
            ((count, FF), bf16, rows_spec(step_rows, FF)),
            ((count, D), f32, rows_spec(step_rows, D)),
        ]
        + [((count, D), bf16, rows_spec(step_rows, D)), ((1, D), f32, whole_spec(1, D))]
        + [(shape, bf16, whole_spec(*shape)) for _, shapes in backs for shape in shapes],
        [
            pltpu.VMEM((D, D), bf16),
            pltpu.VMEM((D, 2 * FF), bf16),
            pltpu.VMEM((FF, D), bf16),
            pltpu.VMEM((D, D), f32),
            pltpu.VMEM((D, 2 * FF), f32),
            pltpu.VMEM((FF, D), f32),
            pltpu.SemaphoreType.DMA,
        ],
        2 * count * (3 * D * D + 8 * D * FF),
        count * D * 16,
    )
    hidden, gated, grad_hidden, grad_mix, gain_mlp_grad = results[:5]
    weight_grads = results[5:]

    grad_blocks = [None] * GROUPS
    grads = []

    def attention_back(at, waits, through):
        order = (ALONG_X, ALONG_Y) if at == 0 else (ALONG_Y, ALONG_X)
        spots, shapes = back_places(D, WIDTH, *order)
        results = call(
            functools.partial(backward_kernel, spots, len(shapes)),
            sequences,
            [
                (me, SMEM),
                (normed, rows_spec(LEN, D)),
                (qkv, group_spec(at, WIDTH)),
                (probs, probs_spec(at)),
                (grad_mix, group_spec(at, EACH * PAIR)),
                (tables, whole_spec(3, LEN, PAIR)),
                (masks, whole_spec(2, PAIR)),
            ],
            [((count, 3 * D), bf16, group_spec(at, WIDTH))]
            + [(shape, bf16, whole_spec(*shape)) for shape in shapes],
            [pltpu.VMEM((D, WIDTH), f32)] + [pltpu.VMEM((LEN, EACH * PAIR), f32)] * 2,
            4 * count * D * WIDTH,
            count * WIDTH * 8,
            waits=waits,
            through=through,
            into=grads,
        )
        results, handed = results if through else (results, [])
        grads[:] = results[:1]
        grad_blocks[at] = results[1:]
        return handed

    last_rows = 256
    halves = 2
    steps = count // last_rows // halves

    def last_part(part, before, waits, through):
        arrays, loads, spots = last()
        part_rows = lambda columns: pl.BlockSpec((last_rows, columns), lambda i: (i + part * steps, 0))
        inputs = (
            [
                (me, SMEM),
                (tokens, part_rows(D)),
                (gain_attn, whole_spec(1, D)),
                (grad_hidden, part_rows(D)),
                (grads[0], part_rows(3 * D)),
            ]
            + [(array, ANYWHERE) for array in arrays]
        )
        return call(
            functools.partial(final_kernel, loads, spots, len(arrays)),
            steps,
            inputs,
            [((count, D), f32, part_rows(D)), ((1, D), f32, whole_spec(1, D))],
            [pltpu.VMEM((D, 3 * D), bf16), pltpu.SemaphoreType.DMA],
            6 * count * D * D // halves,
            count * D * 20 // halves,
            waits=waits,
            through=through,
            into=before,
        )

    def layer_output(waits, through):
        arrays, loads, spots = ends()
        return call(
            functools.partial(output_kernel, loads, spots, len(arrays)),
            count // last_rows,
            [(me, SMEM), (hidden, rows_spec(last_rows, D)), (gated, rows_spec(last_rows, FF))]
            + [(array, ANYWHERE) for array in arrays],
            [((count, D), bf16, rows_spec(last_rows, D))],
            [pltpu.VMEM((FF, D), bf16), pltpu.SemaphoreType.DMA],
            2 * count * FF * D,
            count * D * 12,
            waits=waits,
            through=through,
        )

    if fast:
        (out_keep, out_send), (in_keep, in_send), (mlp_keep, mlp_send) = (
            weight_grads[:2],
            weight_grads[2:4],
            weight_grads[4:],
        )
        out_got, in_got, mlp_got = swap(out_send, CORE), swap(in_send, CORE), swap(mlp_send, CORE)
        in_keep, out_keep, mlp_keep = attention_back(2, [], [in_keep, out_keep, mlp_keep])
        in_keep, in_send = halved(in_keep, in_got)
        out_keep, out_send = halved(out_keep, out_got)
        mlp_keep, mlp_send = halved(mlp_keep, mlp_got)
        in_got, out_got, mlp_got = swap(in_send, ALONG_X), swap(out_send, ALONG_Y), swap(mlp_send, ALONG_Y)
        in_keep, out_keep, mlp_keep = attention_back(1, [], [in_keep, out_keep, mlp_keep])
        in_keep, in_send = halved(in_keep, in_got)
        out_keep, out_send = halved(out_keep, out_got)
        mlp_line = joined_sum(mlp_keep, mlp_got)
        in_got, out_got = swap(in_send, ALONG_Y), swap(out_send, ALONG_X)
        mlp_got = [swap(mlp_line[j], ALONG_Z * j) for j in (1, 2, 3)]
        later_got = [swap(grad_blocks[at][1], CORE) for at in (1, 2)]
        in_keep, out_keep, mlp_own, *later = attention_back(
            0, [mlp_line], [in_keep, out_keep, mlp_line[0], grad_blocks[1][0], grad_blocks[2][0]]
        )
        line = jnp.concatenate([joined_sum(in_keep, in_got), joined_sum(out_keep, out_got)], axis=2)
        line_got = [swap(line[j], ALONG_Z * j) for j in (1, 2, 3)]
        later = [halved(kept, got) for kept, got in zip(later, later_got)]
        later_keep = jnp.concatenate([keep for keep, _ in later], axis=2)
        later_got = swap(jnp.concatenate([send for _, send in later], axis=2), ALONG_X)
        early_got = swap(grad_blocks[0][1], CORE)
        total_mlp = mlp_own.astype(f32)
        for got in mlp_got:
            total_mlp = total_mlp + got.astype(f32)
        rows = total_mlp.shape[0] // 2
        low, high = total_mlp[:rows], total_mlp[rows:]
        mlp_other = swap(jnp.where(bit_of(ALONG_X), low, high).astype(bf16), ALONG_X)
        mlp_own = jnp.where(bit_of(ALONG_X), high, low)
        (tokens_grad, gain_first), (later_keep, early_keep, line_own, mlp_own) = last_part(
            0, [], [], [later_keep, grad_blocks[0][0], line[0], mlp_own]
        )
        later_keep, later_send = halved(later_keep, later_got)
        later_got = swap(later_send, ALONG_Y)
        early_keep, early_send = halved(early_keep, early_got)
        early_got = swap(early_send, ALONG_Y)
        total = line_own.astype(f32)
        for got in line_got:
            total = total + got.astype(f32)
        total_mlp = mlp_own + mlp_other.astype(f32)
        joined_mlp = join_columns(total_mlp)
        joined_rest = join_columns(total)
        (tokens_grad, gain_last), (later_keep, early_keep) = last_part(
            1, [tokens_grad], line_got + [mlp_other], [later_keep, early_keep]
        )
        gains_grad = jnp.concatenate([(gain_first + gain_last).reshape(-1), gain_mlp_grad.reshape(-1)])
        gains_keep, gains_got = swap_half(gains_grad, 2 * ALONG_Z)
        early_keep, early_send = halved(early_keep, early_got)
        early_got = swap(early_send, ALONG_X)
        later_line = joined_sum(later_keep, later_got)
        (output,), (early_keep, gains_keep) = layer_output([later_line], [early_keep, gains_keep])
        gains_share = gains_keep + gains_got
        for bits in (ALONG_Z, ALONG_Y, ALONG_X, CORE):
            gains_keep, gains_got = swap_half(gains_share, bits)
            gains_share = gains_keep + gains_got
        early_line = joined_sum(early_keep, early_got)
        early_later = summed_line(jnp.concatenate([early_line, later_line], axis=2))
        mlp_share = both_columns(joined_mlp, 0, D // 2).reshape(-1)
        in_share = both_columns(joined_rest, 0, FF).reshape(-1)
        out_share = both_columns(joined_rest, FF, FF + D // 2).reshape(-1)
        joined = join_columns(early_later)
        qkv_share = [both_columns(joined, at * 3 * PAIR, (at + 1) * 3 * PAIR) for at in range(GROUPS)]
        qkv_share = jnp.concatenate(qkv_share, axis=1).reshape(24, PAIRS, 3, PAIR)
        qkv_share = qkv_share.transpose(0, 2, 1, 3).reshape(-1)
    else:
        for at in reversed(range(GROUPS)):
            attention_back(at, [], [])
        tokens_grad, gain_first = last_part(0, [], [], [])
        tokens_grad, gain_last = last_part(1, [tokens_grad], [], [])
        (output,) = layer_output([], [])
        add = lambda grad: lax.psum_scatter(
            grad.astype(f32).reshape(-1), "fsdp", scatter_dimension=0, tiled=True
        )
        out_share, in_share, mlp_share = (add(grad) for grad in weight_grads)
        qkv_grad = jnp.concatenate([blocks[0].reshape(D, EACH, 3, PAIR) for blocks in grad_blocks], axis=1)
        qkv_share = add(qkv_grad.transpose(0, 2, 1, 3))
        gains_share = add(jnp.concatenate([gain_first + gain_last, gain_mlp_grad]))
    return (output, tokens_grad, qkv_share, out_share, in_share, mlp_share, gains_share)


def solution(mesh):
    placed = (P("fsdp", None),) + (P("fsdp"),) * 5 + (P("fsdp", None),)
    return jax.shard_map(
        functools.partial(shards, mesh.shape["fsdp"]),
        mesh=mesh,
        in_specs=placed,
        out_specs=(P("fsdp", None),) * 2 + (P("fsdp"),) * 5,
        check_vma=False,
    )
```

```python
import functools

import jax
import jax.numpy as jnp
import numpy as np
from jax import lax
from jax.experimental import pallas as pl
from jax.experimental.pallas import tpu as pltpu
from jax.sharding import PartitionSpec as P

D = 768
HEADS = 12
HEAD = 64
FF = 1152
WIN = 128
LEN = 512
PAIR = 2 * HEAD
PAIRS = HEADS // 2
BLOCK = 128
SPAN = 2 * BLOCK
BLOCKS = LEN // BLOCK
STARTS = tuple(min(max(BLOCK * i - WIN // 2, 0), LEN - SPAN) for i in range(BLOCKS))
GROUPS = 3
EACH = PAIRS // GROUPS
WIDTH = EACH * 3 * PAIR
CORE, ALONG_X, ALONG_Y, ALONG_Z = 1, 2, 4, 8
NOWHERE = (0, 0, 0, 0, 0, 0, 0)
VMEM_LIMIT = 60 * 1024 * 1024
f32 = jnp.float32
bf16 = jnp.bfloat16


def dot_nn(left, right):
    return lax.dot_general(left, right, (((1,), (0,)), ((), ())), preferred_element_type=f32)


def dot_nt(left, right):
    return lax.dot_general(left, right, (((1,), (1,)), ((), ())), preferred_element_type=f32)


def dot_tn(left, right):
    return lax.dot_general(left, right, (((0,), (0,)), ((), ())), preferred_element_type=f32)


def swap(values, bits):
    return lax.ppermute(values, "fsdp", [(i, i ^ bits) for i in range(32)])


def bit_of(bits):
    return (lax.axis_index("fsdp") & bits) != 0


def ordered(bits, mine, other, axis):
    return jnp.where(
        bit_of(bits), jnp.concatenate([other, mine], axis), jnp.concatenate([mine, other], axis)
    )


def after(values, token):
    return jnp.where(token[(0,) * token.ndim].astype(f32) < jnp.inf, values, jnp.zeros_like(values))


def split_columns(shard):
    half = shard.shape[1] // 2
    low, high = shard[:, :half], shard[:, half:]
    other = swap(jnp.where(bit_of(CORE), low, high), CORE)
    return ordered(CORE, jnp.where(bit_of(CORE), high, low), other, 0)


def along_line(own):
    return jnp.stack([own] + [swap(own, ALONG_Z * j) for j in (1, 2, 3)])


def chip_flips(count, first, second):
    return [ALONG_Z * (at % 4) | first * (at // 4 % 2) | second * (at // 8) for at in range(count)]


def swap_half(values, bits):
    half = values.shape[0] // 2
    low, high = values[:half], values[half:]
    other = swap(jnp.where(bit_of(bits), low, high), bits)
    return jnp.where(bit_of(bits), high, low), other


def joined_sum(kept, received):
    return (kept.astype(f32) + received.astype(f32)).astype(bf16)


def halved(kept, received):
    half = kept.shape[0] // 2
    return (
        joined_sum(kept[:half], received[:half]),
        joined_sum(kept[half:], received[half:]),
    )


def summed_line(line):
    total = line[0].astype(f32)
    for j in (1, 2, 3):
        total = total + swap(line[j], ALONG_Z * j).astype(f32)
    return total


def join_columns(total):
    rows = total.shape[0] // 2
    low, high = total[:rows], total[rows:]
    other = swap(jnp.where(bit_of(CORE), low, high), CORE)
    return jnp.where(bit_of(CORE), high, low), other


def both_columns(joined, start, stop):
    mine, other = joined
    return ordered(CORE, mine[:, start:stop], other[:, start:stop], 1)


def place(me_ref, spot):
    flips, shift, rows, row, side, columns, column = spot
    me = me_ref[0]
    return (
        pl.multiple_of(((me ^ flips) >> shift) * rows + row, 16),
        pl.multiple_of(((me & 1) ^ side) * columns + column, 128),
    )


def load_pieces(me_ref, loads, spots, arrays, weights, sem):
    copies = []
    for at, (array, block, start, width, weight) in enumerate(loads):
        piece = arrays[array].at[block, :, pl.ds(start, width)]
        rows = arrays[array].shape[1]
        row, column = place(me_ref, spots[at])
        copy = pltpu.make_async_copy(piece, weights[weight].at[pl.ds(row, rows), pl.ds(column, width)], sem)
        copy.start()
        copies.append(copy)
    return copies


def store_blocks(me_ref, spots, total, outs):
    at = 0
    for out in outs:
        blocks, rows, columns = out.shape
        for block in range(blocks):
            row, column = place(me_ref, spots[at])
            out[block] = total[pl.ds(row, rows), pl.ds(column, columns)].astype(bf16)
            at += 1


def turn(values, tables, sign):
    cosine, sine_up, sine_down = tables
    up = pltpu.roll(values, HEAD // 2, 1)
    down = pltpu.roll(values, PAIR - HEAD // 2, 1)
    if sign > 0:
        return values * cosine + (up * sine_up + down * sine_down)
    return values * cosine - (up * sine_up + down * sine_down)


def norm_of(values):
    centered = values - jnp.mean(values, axis=-1, keepdims=True)
    spread = jnp.mean(centered * centered, axis=-1, keepdims=True)
    scale = lax.rsqrt(spread + 1e-05)
    return centered * scale, scale


def norm_back(grad, normed, scale):
    return scale * (
        grad
        - jnp.mean(grad, axis=-1, keepdims=True)
        - normed * jnp.mean(grad * normed, axis=-1, keepdims=True)
    )


def band(block):
    key = lax.broadcasted_iota(jnp.int32, (SPAN, SPAN), 0) + STARTS[block]
    query = lax.broadcasted_iota(jnp.int32, (SPAN, SPAN), 1) % BLOCK + block * BLOCK
    return jnp.abs(key - query) <= WIN // 2


def both_heads(values, masks_ref):
    return jnp.concatenate([values * masks_ref[0:1, :], values * masks_ref[1:2, :]], axis=0)


def apart(turned):
    nothing = jnp.zeros((HEAD, turned.shape[1]), turned.dtype)
    first = jnp.concatenate([turned[:HEAD], nothing], axis=0)
    second = jnp.concatenate([nothing, turned[HEAD:]], axis=0)
    return jnp.concatenate([first, second], axis=1)


def one_of_each(stacked):
    return jnp.concatenate([stacked[:HEAD, :BLOCK], stacked[HEAD:, BLOCK:]], axis=0)


def turned_windows(values):
    straight = values.T
    shifted = values[STARTS[1] : LEN - STARTS[1]].T
    return [
        straight[:, :SPAN],
        shifted[:, :SPAN],
        shifted[:, BLOCK : BLOCK + SPAN],
        straight[:, LEN - SPAN :],
    ]


def staggered(tiles, first, second, third):
    ones, twos = {}, {}
    for at in range(len(tiles) + 2):
        if at < len(tiles):
            ones[at] = first(*tiles[at])
        if 1 <= at <= len(tiles):
            twos[at - 1] = second(*tiles[at - 1], ones.pop(at - 1))
        if at >= 2:
            third(*tiles[at - 2], twos.pop(at - 2))


def forward_kernel(loads, spots, arrays_n, me_ref, rows_ref, gain_ref, tables_ref, masks_ref, *refs):
    arrays = refs[:arrays_n]
    qkv_ref, probs_ref, mix_ref, *normed_ref, weight, bias, sem = refs[arrays_n:]

    @pl.when(pl.program_id(0) == 0)
    def _():
        copies = load_pieces(me_ref, loads, spots, arrays, [weight], sem)
        for block in range(3):
            bias[block] = jnp.where(band(block if block < 2 else BLOCKS - 1), 0.0, -1e30)
        for copy in copies:
            copy.wait()

    if normed_ref:
        normed, _ = norm_of(rows_ref[...].astype(f32))
        normed_ref[0][...] = (normed * gain_ref[...]).astype(bf16)
        rows_ref = normed_ref[0]
    tables = (tables_ref[0], tables_ref[1], tables_ref[2])

    projected = dot_nn(rows_ref[...], weight[...])
    for pair in range(EACH):
        column = pair * 3 * PAIR
        queries = turn(projected[:, column : column + PAIR], tables, 1)
        key_rows = turn(projected[:, column + PAIR : column + 2 * PAIR], tables, 1)
        qkv_ref[:, column : column + PAIR] = queries.astype(bf16) * bf16(HEAD**-0.5)
        qkv_ref[:, column + PAIR : column + 2 * PAIR] = key_rows.astype(bf16)
        qkv_ref[:, column + 2 * PAIR : column + 3 * PAIR] = projected[
            :, column + 2 * PAIR : column + 3 * PAIR
        ].astype(bf16)

    turned_queries, values = [], []
    for pair in range(EACH):
        column = pair * 3 * PAIR
        turned_queries.append(qkv_ref[:, column : column + PAIR].T)
        values.append(turned_windows(qkv_ref[:, column + 2 * PAIR : column + 3 * PAIR]))
    mixed = [[None] * BLOCKS for _ in range(EACH)]

    def score(pair, block):
        key_column = pair * 3 * PAIR + PAIR
        rows = slice(block * BLOCK, (block + 1) * BLOCK)
        window = slice(STARTS[block], STARTS[block] + SPAN)
        return dot_nn(qkv_ref[window, key_column : key_column + PAIR], apart(turned_queries[pair][:, rows]))

    def weigh(pair, block, scores):
        scores = scores + bias[0 if block == 0 else (2 if block == BLOCKS - 1 else 1)]
        raised = jnp.exp(scores - jnp.max(scores, axis=0, keepdims=True))
        probs = (raised * (1.0 / jnp.sum(raised, axis=0, keepdims=True))).astype(bf16)
        probs_ref[0, 0, pair, block] = probs
        return probs

    def mix(pair, block, probs):
        mixed[pair][block] = one_of_each(dot_nn(values[pair][block], probs)).astype(bf16)
        if block == BLOCKS - 1:
            mix_ref[:, pair * PAIR : (pair + 1) * PAIR] = jnp.concatenate(mixed[pair], axis=1).T

    staggered([(pair, block) for pair in range(EACH) for block in range(BLOCKS)], score, weigh, mix)


def feed_kernel(loads, spots, arrays_n, backs, *refs):
    refs = list(refs)
    take = lambda n: [refs.pop(0) for _ in range(n)]
    (me_ref,) = take(1)
    tokens_ref, cot_ref, gain_ref = take(3)
    (mix_ref,) = take(1)
    arrays = take(arrays_n)
    hidden_ref, gated_ref, grad_hidden_ref = take(3)
    (grad_mix_ref,) = take(1)
    (gain_grad_ref,) = take(1)
    out_grads, in_grads, mlp_grads = (take(len(back[1])) for back in backs)
    w_out, w_in, w_mlp, t_out, t_in, t_mlp, sem = refs
    step = pl.program_id(0)

    @pl.when(step == 0)
    def _():
        copies = load_pieces(me_ref, loads, spots, arrays, [w_out, w_in, w_mlp], sem)
        t_out[...] = jnp.zeros_like(t_out)
        t_in[...] = jnp.zeros_like(t_in)
        t_mlp[...] = jnp.zeros_like(t_mlp)
        gain_grad_ref[...] = jnp.zeros_like(gain_grad_ref)
        for copy in copies:
            copy.wait()

    mixed = mix_ref[...]
    cot = cot_ref[...]
    hidden = tokens_ref[...].astype(f32) + dot_nn(mixed, w_out[...])
    hidden_ref[...] = hidden
    normed, scale = norm_of(hidden)
    gain = gain_ref[...]
    normed_mlp = (normed * gain).astype(bf16)
    grad_gated = dot_nt(cot, w_mlp[...])
    entry = dot_nn(normed_mlp, w_in[:, :FF])
    gate = dot_nn(normed_mlp, w_in[:, FF:])
    below = 0.5 * (1.0 + lax.erf(entry * 0.7071067811865476))
    density = jnp.exp(-0.5 * entry * entry) * 0.3989422804014327
    unit = entry * below
    gated = (unit * gate).astype(bf16)
    gated_ref[...] = gated
    grad_entry = ((below + entry * density) * (gate * grad_gated)).astype(bf16)
    grad_gate = (unit * grad_gated).astype(bf16)
    t_mlp[...] += dot_tn(gated, cot)
    turned = normed_mlp.T
    t_in[:, :FF] += dot_nn(turned, grad_entry)
    t_in[:, FF:] += dot_nn(turned, grad_gate)
    grad_normed = dot_nt(grad_entry, w_in[:, :FF]) + dot_nt(grad_gate, w_in[:, FF:])
    gain_grad_ref[...] += jnp.sum(grad_normed * normed, axis=0, keepdims=True)
    grad_hidden = cot.astype(f32) + norm_back(grad_normed * gain, normed, scale)
    grad_hidden_ref[...] = grad_hidden
    grad_out = grad_hidden.astype(bf16)
    t_out[...] += dot_tn(mixed, grad_out)
    grad_mix_ref[...] = dot_nt(grad_out, w_out[...]).astype(bf16)

    @pl.when(step == pl.num_programs(0) - 1)
    def _():
        store_blocks(me_ref, backs[0][0], t_out, out_grads)
        store_blocks(me_ref, backs[1][0], t_in, in_grads)
        store_blocks(me_ref, backs[2][0], t_mlp, mlp_grads)


def backward_kernel(
    spots, outs_n, me_ref, normed_ref, qkv_ref, probs_ref, grad_mix_ref, tables_ref, masks_ref, *refs
):
    grad_ref = refs[0]
    outs = refs[1 : 1 + outs_n]
    total, grad_keys, grad_values = refs[1 + outs_n :]
    step = pl.program_id(0)

    @pl.when(step == 0)
    def _():
        total[...] = jnp.zeros_like(total)

    tables = (tables_ref[0], tables_ref[1], tables_ref[2])

    grad_keys[...] = jnp.zeros_like(grad_keys)
    grad_values[...] = jnp.zeros_like(grad_values)
    turned_grads, turned_keys = [], []
    for pair in range(EACH):
        column = pair * 3 * PAIR + PAIR
        turned_grads.append(grad_mix_ref[:, pair * PAIR : (pair + 1) * PAIR].T)
        turned_keys.append(turned_windows(qkv_ref[:, column : column + PAIR]))
    grad_queries = [[None] * BLOCKS for _ in range(EACH)]

    def soften(pair, block):
        column = pair * 3 * PAIR + 2 * PAIR
        rows = slice(block * BLOCK, (block + 1) * BLOCK)
        window = slice(STARTS[block], STARTS[block] + SPAN)
        return dot_nn(qkv_ref[window, column : column + PAIR], apart(turned_grads[pair][:, rows]))

    def score(pair, block, grad_soft):
        soft = probs_ref[0, 0, pair, block].astype(f32)
        inner = jnp.sum(soft * grad_soft, axis=0, keepdims=True)
        return (soft * (grad_soft - inner)).astype(bf16)

    def spread(pair, block, grad_scores):
        column = pair * 3 * PAIR
        own = slice(pair * PAIR, (pair + 1) * PAIR)
        rows = slice(block * BLOCK, (block + 1) * BLOCK)
        window = slice(STARTS[block], STARTS[block] + SPAN)
        queries = both_heads(qkv_ref[rows, column : column + PAIR], masks_ref)
        grad_mix = both_heads(grad_mix_ref[rows, own], masks_ref)
        grad_values[window, own] += dot_nn(probs_ref[0, 0, pair, block], grad_mix)
        grad_keys[window, own] += dot_nn(grad_scores, queries)
        grad_queries[pair][block] = one_of_each(dot_nn(turned_keys[pair][block], grad_scores))
        if block == BLOCKS - 1:
            turned = jnp.concatenate(grad_queries[pair], axis=1).T * HEAD**-0.5
            grad_ref[:, column : column + PAIR] = turn(turned, tables, -1).astype(bf16)
            grad_ref[:, column + PAIR : column + 2 * PAIR] = turn(grad_keys[:, own], tables, -1).astype(bf16)
            grad_ref[:, column + 2 * PAIR : column + 3 * PAIR] = grad_values[:, own].astype(bf16)

    staggered([(pair, block) for pair in range(EACH) for block in range(BLOCKS)], soften, score, spread)
    total[...] += dot_tn(normed_ref[...], grad_ref[...])

    @pl.when(step == pl.num_programs(0) - 1)
    def _():
        store_blocks(me_ref, spots, total, outs)


def final_kernel(loads, spots, arrays_n, me_ref, tokens_ref, gain_ref, grad_hidden_ref, grad_ref, *refs):
    arrays = refs[:arrays_n]
    tokens_grad_ref, gain_grad_ref, weight, sem = refs[arrays_n:]

    @pl.when(pl.program_id(0) == 0)
    def _():
        copies = load_pieces(me_ref, loads, spots, arrays, [weight], sem)
        gain_grad_ref[...] = jnp.zeros_like(gain_grad_ref)
        for copy in copies:
            copy.wait()

    grad_normed = dot_nt(grad_ref[...], weight[...])
    normed, scale = norm_of(tokens_ref[...].astype(f32))
    gain_grad_ref[...] += jnp.sum(grad_normed * normed, axis=0, keepdims=True)
    tokens_grad_ref[...] = grad_hidden_ref[...] + norm_back(grad_normed * gain_ref[...], normed, scale)


def output_kernel(loads, spots, arrays_n, me_ref, hidden_ref, gated_ref, *refs):
    arrays = refs[:arrays_n]
    output_ref, weight, sem = refs[-3:]

    @pl.when(pl.program_id(0) == 0)
    def _():
        for copy in load_pieces(me_ref, loads, spots, arrays, [weight], sem):
            copy.wait()

    output_ref[...] = (hidden_ref[...] + dot_nn(gated_ref[...], weight[...])).astype(bf16)


SMEM = pl.BlockSpec(memory_space=pltpu.SMEM)
ANYWHERE = pl.BlockSpec(memory_space=pl.ANY)


def rows_spec(rows, columns):
    return pl.BlockSpec((rows, columns), lambda i: (i, 0))


def whole_spec(*shape):
    return pl.BlockSpec(shape, lambda i: (0,) * len(shape))


def call(kernel, steps, inputs, outputs, scratch, flops, nbytes, waits=(), through=(), into=()):
    extra = list(waits) + list(through) + list(into)
    n_in, n_out, n_through = len(inputs), len(outputs), len(through)
    begin = n_in + len(extra)

    def trimmed(*refs):
        kernel(*refs[:n_in], *refs[begin : begin + n_out], *refs[begin + n_out + n_through :])

    aliases = {n_in + len(waits) + at: n_out + at for at in range(n_through)}
    aliases.update({n_in + len(waits) + n_through + at: at for at in range(len(into))})
    results = pl.pallas_call(
        trimmed,
        grid=(steps,),
        in_specs=[spec for _, spec in inputs] + [ANYWHERE] * len(extra),
        out_specs=[spec for _, _, spec in outputs] + [ANYWHERE] * n_through,
        out_shape=[jax.ShapeDtypeStruct(shape, dtype) for shape, dtype, _ in outputs]
        + [jax.ShapeDtypeStruct(array.shape, array.dtype) for array in through],
        scratch_shapes=scratch,
        input_output_aliases=aliases,
        compiler_params=pltpu.CompilerParams(
            dimension_semantics=("arbitrary",), vmem_limit_bytes=VMEM_LIMIT
        ),
        cost_estimate=pl.CostEstimate(flops=int(flops), bytes_accessed=int(nbytes), transcendentals=0),
    )(*[array for array, _ in inputs], *extra)
    if not through:
        return results
    return results[:n_out], results[n_out:]


def rope_constants():
    inverse = 10000.0 ** (-np.arange(0, HEAD, 2, dtype=np.float64) / HEAD)
    angles = np.arange(LEN, dtype=np.float64)[:, None] * inverse[None, :]
    angles = np.concatenate([angles] * 4, axis=-1)
    upper = (np.arange(PAIR) % HEAD >= HEAD // 2)[None, :]
    sine = np.sin(angles)
    return np.stack([np.cos(angles), np.where(upper, sine, 0.0), np.where(upper, 0.0, -sine)]).astype(
        np.float32
    )


def spread_loads(arrays, flips, start, width, weight, column):
    loads, spots = [], []
    for index, blocks, first_chip, other in arrays:
        for block in range(blocks):
            loads.append((index, block, start, width, weight))
            spots.append((flips[first_chip + block], 1, 48, 0, other, width, column))
    return loads, spots


def gather_weights(qkv_weight, out_weight, in_weight, mlp_weight, norm_gains):
    by_pair = qkv_weight.reshape(24, 3, PAIRS, PAIR).transpose(0, 2, 1, 3).reshape(24, PAIRS, 3 * PAIR)
    gain_row = jnp.pad(norm_gains.reshape(1, 48), ((0, 23), (0, 80)))
    early = split_columns(
        jnp.concatenate([by_pair[:, 0], gain_row, by_pair[:, 1], gain_row], axis=1)
    )
    later = split_columns(
        jnp.concatenate([by_pair[:, 2], by_pair[:, 4], by_pair[:, 3], by_pair[:, 5]], axis=1)
    )
    own_in = split_columns(after(in_weight.reshape(24, 2 * FF), early))
    own_out = split_columns(after(out_weight.reshape(24, D), early))
    own_mlp = split_columns(after(mlp_weight.reshape(36, D), early))
    own_mlp = ordered(ALONG_X, own_mlp, swap(own_mlp, ALONG_X), 0)

    line = along_line(early)
    plane = jnp.concatenate([line, swap(line, ALONG_X)])
    far = swap(plane, ALONG_Y)
    first_arrays = [plane, far, swap(plane, CORE), swap(far, CORE)]
    chips = chip_flips(16, ALONG_X, ALONG_Y)
    slots = [(0, 8, 0, 0), (1, 8, 8, 0), (2, 8, 0, 1), (3, 8, 8, 1)]
    first = (first_arrays, *spread_loads(slots, chips, 0, 3 * PAIR, 0, 0))
    scales = jnp.concatenate([plane, far])[:, :, 3 * PAIR : 3 * PAIR + 48]
    scales = jnp.concatenate([scales[:, 0], scales[:, 24]], axis=1)
    held = (lax.axis_index("fsdp") ^ np.asarray(chips, np.int32)) // 2
    spot = held[None, :] == np.arange(16, dtype=np.int32)[:, None]
    gains = dot_nn(spot.astype(bf16), scales).reshape(-1)

    line = along_line(after(later, line))
    early_plane = plane
    plane = jnp.concatenate([line, swap(line, ALONG_Y)])
    far = swap(plane, ALONG_X)
    other_arrays = [plane, far, swap(plane, CORE), swap(far, CORE)]
    chips = chip_flips(16, ALONG_Y, ALONG_X)
    others = [
        (other_arrays, *spread_loads(slots, chips, 3 * PAIR * at, 3 * PAIR, 0, 0)) for at in range(2)
    ]

    rows = own_mlp.shape[0] // 3
    thirds = [own_mlp[rows * i : rows * (i + 1)] for i in range(3)]
    own = after(jnp.concatenate([own_in, own_out] + thirds, axis=1), early_plane)
    start_out, start_mlp = FF, FF + D // 2
    parts = [own] + [swap(own, ALONG_Z * j) for j in (1, 2, 3)]
    rest_arrays = []

    def near(own_mlp):
        thirds = [own_mlp[rows * i : rows * (i + 1)] for i in range(3)]
        own = jnp.concatenate([own_in, own_out] + thirds, axis=1)
        line = jnp.stack([own] + parts[1:])
        beside = swap(line[:, :, :start_out], ALONG_X), swap(line[:, :, start_out:], ALONG_Y)
        return line, line[:, :, :start_mlp], beside

    def far(line, head, beside):
        beside_in, beside_rest = beside
        beside_out = beside_rest[:, :, : D // 2]
        mlp = jnp.concatenate([line[:, :, start_mlp:], beside_rest[:, :, D // 2 :]])
        far_in = swap(jnp.concatenate([head[:, :, :start_out], beside_in]), ALONG_Y)
        far_out = swap(jnp.concatenate([head[:, :, start_out:], beside_out]), ALONG_X)
        return (beside_in, beside_out), (far_in, far_out), mlp, swap(mlp, CORE)

    def across(head, beside, beyond, mlp, mlp_other):
        all_in = jnp.concatenate([head[:, :, :start_out], beside[0], beyond[0]])
        all_out = jnp.concatenate([head[:, :, start_out:], beside[1], beyond[1]])
        both = jnp.concatenate([all_in, all_out], axis=2)
        rest_arrays.extend([both, swap(both, CORE), mlp, mlp_other])

    in_loads, in_spots = spread_loads(
        [(0, 16, 0, 0), (1, 16, 0, 1)], chip_flips(16, ALONG_X, ALONG_Y), 0, FF, 1, 0
    )
    out_loads, out_spots = spread_loads(
        [(0, 16, 0, 0), (1, 16, 0, 1)], chip_flips(16, ALONG_Y, ALONG_X), start_out, D // 2, 0, 0
    )
    mlp_loads, mlp_spots = [], []
    for other in (0, 1):
        for block, flips in enumerate(chip_flips(8, ALONG_Y, 0)):
            for third in range(3):
                mlp_loads.append((2 + other, block, third * (D // 2), D // 2, 2))
                mlp_spots.append((flips, 2, 144, third * 48, other, D // 2, 0))
    rest = (rest_arrays, out_loads + in_loads + mlp_loads, out_spots + in_spots + mlp_spots)

    last_loads, last_spots = list(first[1]), list(first[2])
    for group in range(2):
        column = WIDTH * (group + 1)
        more = spread_loads(slots, chips, 3 * PAIR * group, 3 * PAIR, 0, column)
        last_loads += [(load[0] + 4,) + load[1:] for load in more[0]]
        last_spots += more[1]
    end_loads = [(load[0] - 2,) + load[1:4] + (0,) for load in mlp_loads]
    last = lambda: (first_arrays + other_arrays, last_loads, last_spots)
    ends = lambda: (rest_arrays[2:], end_loads, mlp_spots)
    return gains, [first] + others, rest, last, ends, (own_mlp, parts[1:], near, far, across)


def gather_simply(qkv_weight, out_weight, in_weight, mlp_weight, norm_gains):
    whole = lambda w: lax.all_gather(w, "fsdp", axis=0, tiled=True)
    by_pair = whole(qkv_weight).reshape(D, 3, PAIRS, PAIR).transpose(0, 2, 1, 3)
    w_qkv = by_pair.reshape(1, D, 3 * D)
    w_in, w_out = whole(in_weight).reshape(1, D, 2 * FF), whole(out_weight).reshape(1, D, D)
    w_mlp = whole(mlp_weight).reshape(1, FF, D)
    groups = [([w_qkv], [(0, 0, at * WIDTH, WIDTH, 0)], [NOWHERE]) for at in range(GROUPS)]
    rest = (
        [w_out, w_in, w_mlp],
        [(0, 0, 0, D, 0), (1, 0, 0, 2 * FF, 1), (2, 0, 0, D, 2)],
        [NOWHERE] * 3,
    )
    last = lambda: ([w_qkv], [(0, 0, 0, 3 * D, 0)], [NOWHERE])
    ends = lambda: ([w_mlp], [(0, 0, 0, D, 0)], [NOWHERE])
    return whole(norm_gains), groups, rest, last, ends, None


def shards(devices, tokens, qkv_weight, out_weight, in_weight, mlp_weight, norm_gains, cotangent):
    count = tokens.shape[0]
    sequences = count // LEN
    fast = devices == 32
    gather = gather_weights if fast else gather_simply
    gains, groups, rest, last, ends, rounds = gather(
        qkv_weight, out_weight, in_weight, mlp_weight, norm_gains
    )
    gains = gains.astype(f32)
    gain_attn, gain_mlp = gains[:D].reshape(1, D), gains[D:].reshape(1, D)
    me = lax.axis_index("fsdp").astype(jnp.int32).reshape(1)

    def back_places(rows, columns, first, second):
        if not fast:
            return [NOWHERE], [(1, rows, columns)]
        half = columns // 2
        blocks = 8 if second is None else 16
        rows = rows // blocks
        spots = [
            (flips, 2 if second is None else 1, rows, 0, other, half, 0)
            for other in (0, 1)
            for flips in chip_flips(blocks, first, second or 0)
        ]
        return spots, [(blocks, rows, half)] * 2

    tables = jnp.asarray(rope_constants())
    masks = np.arange(PAIR)[None, :] // HEAD == np.arange(2)[:, None]
    masks = jnp.asarray(masks.astype(np.float32)).astype(bf16)
    probs_shape = (GROUPS, sequences, EACH, BLOCKS, SPAN, SPAN)
    probs_spec = lambda at: pl.BlockSpec((1, 1) + probs_shape[2:], lambda i: (at, i, 0, 0, 0, 0))
    group_spec = lambda at, columns: pl.BlockSpec((LEN, columns), lambda i: (i, at))

    kept = []

    def forward(at, waits, through):
        arrays, loads, spots = groups[at]
        outputs = [
            ((count, 3 * D), bf16, group_spec(at, WIDTH)),
            (probs_shape, bf16, probs_spec(at)),
            ((count, D), bf16, group_spec(at, EACH * PAIR)),
        ]
        if at == 0:
            outputs.append(((count, D), bf16, rows_spec(LEN, D)))
        results = call(
            functools.partial(forward_kernel, loads, spots, len(arrays)),
            sequences,
            [
                (me, SMEM),
                (kept[3] if kept else tokens, rows_spec(LEN, D)),
                (gain_attn, whole_spec(1, D)),
                (tables, whole_spec(3, LEN, PAIR)),
                (masks, whole_spec(2, PAIR)),
            ]
            + [(array, ANYWHERE) for array in arrays],
            outputs,
            [
                pltpu.VMEM((D, WIDTH), bf16),
                pltpu.VMEM((3, SPAN, SPAN), f32),
                pltpu.SemaphoreType.DMA,
            ],
            4 * count * D * WIDTH,
            count * WIDTH * 8,
            waits=waits,
            through=through,
            into=kept[:3],
        )
        results, handed = results if through else (results, [])
        kept[: len(results)] = results
        return handed

    if fast:
        own_mlp, parts, near, far, across = rounds
        (own_mlp,) = forward(0, [], [own_mlp])
        line, head, beside = near(own_mlp)
        (head,) = forward(1, parts, [head])
        beside, beyond, mlp, mlp_other = far(line, head, beside)
        (head,) = forward(2, list(beside), [head])
        across(head, beside, beyond, mlp, mlp_other)
    else:
        for at in range(GROUPS):
            forward(at, [], [])
    qkv, probs, mix, normed = kept

    step_rows = 256
    arrays, loads, spots = rest
    backs = (
        back_places(D, D, ALONG_X, ALONG_Y),
        back_places(D, 2 * FF, ALONG_Y, ALONG_X),
        back_places(FF, D, ALONG_Y, None),
    )
    results = call(
        functools.partial(feed_kernel, loads, spots, len(arrays), backs),
        count // step_rows,
        [(me, SMEM)]
        + [
            (tokens, rows_spec(step_rows, D)),
            (cotangent, rows_spec(step_rows, D)),
            (gain_mlp, whole_spec(1, D)),
        ]
        + [(mix, rows_spec(step_rows, D))]
        + [(array, ANYWHERE) for array in arrays],
        [
            ((count, D), f32, rows_spec(step_rows, D)),
            ((count, FF), bf16, rows_spec(step_rows, FF)),
            ((count, D), f32, rows_spec(step_rows, D)),
        ]
        + [((count, D), bf16, rows_spec(step_rows, D)), ((1, D), f32, whole_spec(1, D))]
        + [(shape, bf16, whole_spec(*shape)) for _, shapes in backs for shape in shapes],
        [
            pltpu.VMEM((D, D), bf16),
            pltpu.VMEM((D, 2 * FF), bf16),
            pltpu.VMEM((FF, D), bf16),
            pltpu.VMEM((D, D), f32),
            pltpu.VMEM((D, 2 * FF), f32),
            pltpu.VMEM((FF, D), f32),
            pltpu.SemaphoreType.DMA,
        ],
        2 * count * (3 * D * D + 8 * D * FF),
        count * D * 16,
    )
    hidden, gated, grad_hidden, grad_mix, gain_mlp_grad = results[:5]
    weight_grads = results[5:]

    grad_blocks = [None] * GROUPS
    grads = []

    def attention_back(at, waits, through):
        order = (ALONG_X, ALONG_Y) if at == 0 else (ALONG_Y, ALONG_X)
        spots, shapes = back_places(D, WIDTH, *order)
        results = call(
            functools.partial(backward_kernel, spots, len(shapes)),
            sequences,
            [
                (me, SMEM),
                (normed, rows_spec(LEN, D)),
                (qkv, group_spec(at, WIDTH)),
                (probs, probs_spec(at)),
                (grad_mix, group_spec(at, EACH * PAIR)),
                (tables, whole_spec(3, LEN, PAIR)),
                (masks, whole_spec(2, PAIR)),
            ],
            [((count, 3 * D), bf16, group_spec(at, WIDTH))]
            + [(shape, bf16, whole_spec(*shape)) for shape in shapes],
            [pltpu.VMEM((D, WIDTH), f32)] + [pltpu.VMEM((LEN, EACH * PAIR), f32)] * 2,
            4 * count * D * WIDTH,
            count * WIDTH * 8,
            waits=waits,
            through=through,
            into=grads,
        )
        results, handed = results if through else (results, [])
        grads[:] = results[:1]
        grad_blocks[at] = results[1:]
        return handed

    last_rows = 256
    halves = 2
    steps = count // last_rows // halves

    def last_part(part, before, waits, through):
        arrays, loads, spots = last()
        part_rows = lambda columns: pl.BlockSpec((last_rows, columns), lambda i: (i + part * steps, 0))
        inputs = (
            [
                (me, SMEM),
                (tokens, part_rows(D)),
                (gain_attn, whole_spec(1, D)),
                (grad_hidden, part_rows(D)),
                (grads[0], part_rows(3 * D)),
            ]
            + [(array, ANYWHERE) for array in arrays]
        )
        return call(
            functools.partial(final_kernel, loads, spots, len(arrays)),
            steps,
            inputs,
            [((count, D), f32, part_rows(D)), ((1, D), f32, whole_spec(1, D))],
            [pltpu.VMEM((D, 3 * D), bf16), pltpu.SemaphoreType.DMA],
            6 * count * D * D // halves,
            count * D * 20 // halves,
            waits=waits,
            through=through,
            into=before,
        )

    def layer_output(waits, through):
        arrays, loads, spots = ends()
        return call(
            functools.partial(output_kernel, loads, spots, len(arrays)),
            count // last_rows,
            [(me, SMEM), (hidden, rows_spec(last_rows, D)), (gated, rows_spec(last_rows, FF))]
            + [(array, ANYWHERE) for array in arrays],
            [((count, D), bf16, rows_spec(last_rows, D))],
            [pltpu.VMEM((FF, D), bf16), pltpu.SemaphoreType.DMA],
            2 * count * FF * D,
            count * D * 12,
            waits=waits,
            through=through,
        )

    if fast:
        (out_keep, out_send), (in_keep, in_send), (mlp_keep, mlp_send) = (
            weight_grads[:2],
            weight_grads[2:4],
            weight_grads[4:],
        )
        out_got, in_got, mlp_got = swap(out_send, CORE), swap(in_send, CORE), swap(mlp_send, CORE)
        in_keep, out_keep, mlp_keep = attention_back(2, [], [in_keep, out_keep, mlp_keep])
        in_keep, in_send = halved(in_keep, in_got)
        out_keep, out_send = halved(out_keep, out_got)
        mlp_keep, mlp_send = halved(mlp_keep, mlp_got)
        in_got, out_got, mlp_got = swap(in_send, ALONG_X), swap(out_send, ALONG_Y), swap(mlp_send, ALONG_Y)
        in_keep, out_keep, mlp_keep = attention_back(1, [], [in_keep, out_keep, mlp_keep])
        in_keep, in_send = halved(in_keep, in_got)
        out_keep, out_send = halved(out_keep, out_got)
        mlp_line = joined_sum(mlp_keep, mlp_got)
        in_got, out_got = swap(in_send, ALONG_Y), swap(out_send, ALONG_X)
        mlp_got = [swap(mlp_line[j], ALONG_Z * j) for j in (1, 2, 3)]
        later_got = [swap(grad_blocks[at][1], CORE) for at in (1, 2)]
        in_keep, out_keep, mlp_own, *later = attention_back(
            0, [mlp_line], [in_keep, out_keep, mlp_line[0], grad_blocks[1][0], grad_blocks[2][0]]
        )
        line = jnp.concatenate([joined_sum(in_keep, in_got), joined_sum(out_keep, out_got)], axis=2)
        line_got = [swap(line[j], ALONG_Z * j) for j in (1, 2, 3)]
        later = [halved(kept, got) for kept, got in zip(later, later_got)]
        later_keep = jnp.concatenate([keep for keep, _ in later], axis=2)
        later_got = swap(jnp.concatenate([send for _, send in later], axis=2), ALONG_X)
        early_got = swap(grad_blocks[0][1], CORE)
        total_mlp = mlp_own.astype(f32)
        for got in mlp_got:
            total_mlp = total_mlp + got.astype(f32)
        rows = total_mlp.shape[0] // 2
        low, high = total_mlp[:rows], total_mlp[rows:]
        mlp_other = swap(jnp.where(bit_of(ALONG_X), low, high).astype(bf16), ALONG_X)
        mlp_own = jnp.where(bit_of(ALONG_X), high, low)
        (tokens_grad, gain_first), (later_keep, early_keep) = last_part(
            0, [], [], [later_keep, grad_blocks[0][0]]
        )
        later_keep, later_send = halved(later_keep, later_got)
        later_got = swap(later_send, ALONG_Y)
        early_keep, early_send = halved(early_keep, early_got)
        early_got = swap(early_send, ALONG_Y)
        (tokens_grad, gain_last), (later_keep, early_keep) = last_part(
            1, [tokens_grad], [], [later_keep, early_keep]
        )
        gains_grad = jnp.concatenate([(gain_first + gain_last).reshape(-1), gain_mlp_grad.reshape(-1)])
        gains_keep, gains_got = swap_half(gains_grad, 2 * ALONG_Z)
        early_keep, early_send = halved(early_keep, early_got)
        early_got = swap(early_send, ALONG_X)
        later_line = joined_sum(later_keep, later_got)
        (output,), (early_keep, line_own, mlp_own) = layer_output(
            [later_line, gains_got], [early_keep, line[0], mlp_own]
        )
        total = line_own.astype(f32)
        for got in line_got:
            total = total + got.astype(f32)
        total_mlp = mlp_own + mlp_other.astype(f32)
        joined_mlp = join_columns(total_mlp)
        joined_rest = join_columns(total)
        early_line = joined_sum(early_keep, early_got)
        gains_share = after(gains_keep + gains_got, early_line)
        for bits in (ALONG_Z, ALONG_Y, ALONG_X, CORE):
            gains_keep, gains_got = swap_half(gains_share, bits)
            gains_share = gains_keep + gains_got
        early_later = summed_line(jnp.concatenate([early_line, later_line], axis=2))
        mlp_share = both_columns(joined_mlp, 0, D // 2).reshape(-1)
        in_share = both_columns(joined_rest, 0, FF).reshape(-1)
        out_share = both_columns(joined_rest, FF, FF + D // 2).reshape(-1)
        joined = join_columns(early_later)
        qkv_share = [both_columns(joined, at * 3 * PAIR, (at + 1) * 3 * PAIR) for at in range(GROUPS)]
        qkv_share = jnp.concatenate(qkv_share, axis=1).reshape(24, PAIRS, 3, PAIR)
        qkv_share = qkv_share.transpose(0, 2, 1, 3).reshape(-1)
    else:
        for at in reversed(range(GROUPS)):
            attention_back(at, [], [])
        tokens_grad, gain_first = last_part(0, [], [], [])
        tokens_grad, gain_last = last_part(1, [tokens_grad], [], [])
        (output,) = layer_output([], [])
        add = lambda grad: lax.psum_scatter(
            grad.astype(f32).reshape(-1), "fsdp", scatter_dimension=0, tiled=True
        )
        out_share, in_share, mlp_share = (add(grad) for grad in weight_grads)
        qkv_grad = jnp.concatenate([blocks[0].reshape(D, EACH, 3, PAIR) for blocks in grad_blocks], axis=1)
        qkv_share = add(qkv_grad.transpose(0, 2, 1, 3))
        gains_share = add(jnp.concatenate([gain_first + gain_last, gain_mlp_grad]))
    return (output, tokens_grad, qkv_share, out_share, in_share, mlp_share, gains_share)


def solution(mesh):
    placed = (P("fsdp", None),) + (P("fsdp"),) * 5 + (P("fsdp", None),)
    return jax.shard_map(
        functools.partial(shards, mesh.shape["fsdp"]),
        mesh=mesh,
        in_specs=placed,
        out_specs=(P("fsdp", None),) * 2 + (P("fsdp"),) * 5,
        check_vma=False,
    )
```

```python
import functools

import jax
import jax.numpy as jnp
import numpy as np
from jax import lax
from jax.experimental import pallas as pl
from jax.experimental.pallas import tpu as pltpu
from jax.sharding import PartitionSpec as P

D = 768
HEADS = 12
HEAD = 64
FF = 1152
WIN = 128
LEN = 512
PAIR = 2 * HEAD
PAIRS = HEADS // 2
BLOCK = 128
SPAN = 2 * BLOCK
BLOCKS = LEN // BLOCK
STARTS = tuple(min(max(BLOCK * i - WIN // 2, 0), LEN - SPAN) for i in range(BLOCKS))
GROUPS = 3
EACH = PAIRS // GROUPS
WIDTH = EACH * 3 * PAIR
CORE, ALONG_X, ALONG_Y, ALONG_Z = 1, 2, 4, 8
NOWHERE = (0, 0, 0, 0, 0, 0, 0)
VMEM_LIMIT = 60 * 1024 * 1024
f32 = jnp.float32
bf16 = jnp.bfloat16


def dot_nn(left, right):
    return lax.dot_general(left, right, (((1,), (0,)), ((), ())), preferred_element_type=f32)


def dot_nt(left, right):
    return lax.dot_general(left, right, (((1,), (1,)), ((), ())), preferred_element_type=f32)


def dot_tn(left, right):
    return lax.dot_general(left, right, (((0,), (0,)), ((), ())), preferred_element_type=f32)


def swap(values, bits):
    return lax.ppermute(values, "fsdp", [(i, i ^ bits) for i in range(32)])


def bit_of(bits):
    return (lax.axis_index("fsdp") & bits) != 0


def ordered(bits, mine, other, axis):
    return jnp.where(
        bit_of(bits), jnp.concatenate([other, mine], axis), jnp.concatenate([mine, other], axis)
    )


def after(values, token):
    return jnp.where(token[(0,) * token.ndim].astype(f32) < jnp.inf, values, jnp.zeros_like(values))


def split_columns(shard):
    half = shard.shape[1] // 2
    low, high = shard[:, :half], shard[:, half:]
    other = swap(jnp.where(bit_of(CORE), low, high), CORE)
    return ordered(CORE, jnp.where(bit_of(CORE), high, low), other, 0)


def along_line(own):
    return jnp.stack([own] + [swap(own, ALONG_Z * j) for j in (1, 2, 3)])


def chip_flips(count, first, second):
    return [ALONG_Z * (at % 4) | first * (at // 4 % 2) | second * (at // 8) for at in range(count)]


def swap_half(values, bits):
    half = values.shape[0] // 2
    low, high = values[:half], values[half:]
    other = swap(jnp.where(bit_of(bits), low, high), bits)
    return jnp.where(bit_of(bits), high, low), other


def joined_sum(kept, received):
    return (kept.astype(f32) + received.astype(f32)).astype(bf16)


def halved(kept, received):
    half = kept.shape[0] // 2
    return (
        joined_sum(kept[:half], received[:half]),
        joined_sum(kept[half:], received[half:]),
    )


def summed_line(line):
    total = line[0].astype(f32)
    for j in (1, 2, 3):
        total = total + swap(line[j], ALONG_Z * j).astype(f32)
    return total


def join_columns(total):
    rows = total.shape[0] // 2
    low, high = total[:rows], total[rows:]
    other = swap(jnp.where(bit_of(CORE), low, high), CORE)
    return jnp.where(bit_of(CORE), high, low), other


def both_columns(joined, start, stop):
    mine, other = joined
    return ordered(CORE, mine[:, start:stop], other[:, start:stop], 1)


def place(me_ref, spot):
    flips, shift, rows, row, side, columns, column = spot
    me = me_ref[0]
    return (
        pl.multiple_of(((me ^ flips) >> shift) * rows + row, 16),
        pl.multiple_of(((me & 1) ^ side) * columns + column, 128),
    )


def load_pieces(me_ref, loads, spots, arrays, weights, sem):
    copies = []
    for at, (array, block, start, width, weight) in enumerate(loads):
        piece = arrays[array].at[block, :, pl.ds(start, width)]
        rows = arrays[array].shape[1]
        row, column = place(me_ref, spots[at])
        copy = pltpu.make_async_copy(piece, weights[weight].at[pl.ds(row, rows), pl.ds(column, width)], sem)
        copy.start()
        copies.append(copy)
    return copies


def store_blocks(me_ref, spots, total, outs):
    at = 0
    for out in outs:
        blocks, rows, columns = out.shape
        for block in range(blocks):
            row, column = place(me_ref, spots[at])
            out[block] = total[pl.ds(row, rows), pl.ds(column, columns)].astype(bf16)
            at += 1


def turn(values, tables, sign):
    cosine, sine_up, sine_down = tables
    up = pltpu.roll(values, HEAD // 2, 1)
    down = pltpu.roll(values, PAIR - HEAD // 2, 1)
    if sign > 0:
        return values * cosine + (up * sine_up + down * sine_down)
    return values * cosine - (up * sine_up + down * sine_down)


def norm_of(values):
    centered = values - jnp.mean(values, axis=-1, keepdims=True)
    spread = jnp.mean(centered * centered, axis=-1, keepdims=True)
    scale = lax.rsqrt(spread + 1e-05)
    return centered * scale, scale


def norm_back(grad, normed, scale):
    return scale * (
        grad
        - jnp.mean(grad, axis=-1, keepdims=True)
        - normed * jnp.mean(grad * normed, axis=-1, keepdims=True)
    )


def band(block):
    key = lax.broadcasted_iota(jnp.int32, (SPAN, SPAN), 0) + STARTS[block]
    query = lax.broadcasted_iota(jnp.int32, (SPAN, SPAN), 1) % BLOCK + block * BLOCK
    return jnp.abs(key - query) <= WIN // 2


def both_heads(values, masks_ref):
    return jnp.concatenate([values * masks_ref[0:1, :], values * masks_ref[1:2, :]], axis=0)


def apart(turned):
    nothing = jnp.zeros((HEAD, turned.shape[1]), turned.dtype)
    first = jnp.concatenate([turned[:HEAD], nothing], axis=0)
    second = jnp.concatenate([nothing, turned[HEAD:]], axis=0)
    return jnp.concatenate([first, second], axis=1)


def one_of_each(stacked):
    return jnp.concatenate([stacked[:HEAD, :BLOCK], stacked[HEAD:, BLOCK:]], axis=0)


def turned_windows(values):
    straight = values.T
    shifted = values[STARTS[1] : LEN - STARTS[1]].T
    return [
        straight[:, :SPAN],
        shifted[:, :SPAN],
        shifted[:, BLOCK : BLOCK + SPAN],
        straight[:, LEN - SPAN :],
    ]


def staggered(tiles, first, second, third):
    ones, twos = {}, {}
    for at in range(len(tiles) + 2):
        if at < len(tiles):
            ones[at] = first(*tiles[at])
        if 1 <= at <= len(tiles):
            twos[at - 1] = second(*tiles[at - 1], ones.pop(at - 1))
        if at >= 2:
            third(*tiles[at - 2], twos.pop(at - 2))


def forward_kernel(loads, spots, arrays_n, me_ref, rows_ref, gain_ref, tables_ref, masks_ref, *refs):
    arrays = refs[:arrays_n]
    qkv_ref, probs_ref, mix_ref, *normed_ref, weight, bias, sem = refs[arrays_n:]

    @pl.when(pl.program_id(0) == 0)
    def _():
        copies = load_pieces(me_ref, loads, spots, arrays, [weight], sem)
        for block in range(3):
            bias[block] = jnp.where(band(block if block < 2 else BLOCKS - 1), 0.0, -1e30)
        for copy in copies:
            copy.wait()

    if normed_ref:
        normed, _ = norm_of(rows_ref[...].astype(f32))
        normed_ref[0][...] = (normed * gain_ref[...]).astype(bf16)
        rows_ref = normed_ref[0]
    tables = (tables_ref[0], tables_ref[1], tables_ref[2])

    projected = dot_nn(rows_ref[...], weight[...])
    for pair in range(EACH):
        column = pair * 3 * PAIR
        queries = turn(projected[:, column : column + PAIR], tables, 1)
        key_rows = turn(projected[:, column + PAIR : column + 2 * PAIR], tables, 1)
        qkv_ref[:, column : column + PAIR] = queries.astype(bf16) * bf16(HEAD**-0.5)
        qkv_ref[:, column + PAIR : column + 2 * PAIR] = key_rows.astype(bf16)
        qkv_ref[:, column + 2 * PAIR : column + 3 * PAIR] = projected[
            :, column + 2 * PAIR : column + 3 * PAIR
        ].astype(bf16)

    turned_queries, values = [], []
    for pair in range(EACH):
        column = pair * 3 * PAIR
        turned_queries.append(qkv_ref[:, column : column + PAIR].T)
        values.append(turned_windows(qkv_ref[:, column + 2 * PAIR : column + 3 * PAIR]))
    mixed = [[None] * BLOCKS for _ in range(EACH)]

    def score(pair, block):
        key_column = pair * 3 * PAIR + PAIR
        rows = slice(block * BLOCK, (block + 1) * BLOCK)
        window = slice(STARTS[block], STARTS[block] + SPAN)
        return dot_nn(qkv_ref[window, key_column : key_column + PAIR], apart(turned_queries[pair][:, rows]))

    def weigh(pair, block, scores):
        scores = scores + bias[0 if block == 0 else (2 if block == BLOCKS - 1 else 1)]
        raised = jnp.exp(scores - jnp.max(scores, axis=0, keepdims=True))
        probs = (raised * (1.0 / jnp.sum(raised, axis=0, keepdims=True))).astype(bf16)
        probs_ref[0, 0, pair, block] = probs
        return probs

    def mix(pair, block, probs):
        mixed[pair][block] = one_of_each(dot_nn(values[pair][block], probs)).astype(bf16)
        if block == BLOCKS - 1:
            mix_ref[:, pair * PAIR : (pair + 1) * PAIR] = jnp.concatenate(mixed[pair], axis=1).T

    staggered([(pair, block) for pair in range(EACH) for block in range(BLOCKS)], score, weigh, mix)


def feed_kernel(loads, spots, arrays_n, backs, *refs):
    refs = list(refs)
    take = lambda n: [refs.pop(0) for _ in range(n)]
    (me_ref,) = take(1)
    tokens_ref, cot_ref, gain_ref = take(3)
    (mix_ref,) = take(1)
    arrays = take(arrays_n)
    hidden_ref, gated_ref, grad_hidden_ref = take(3)
    (grad_mix_ref,) = take(1)
    (gain_grad_ref,) = take(1)
    out_grads, in_grads, mlp_grads = (take(len(back[1])) for back in backs)
    w_out, w_in, w_mlp, t_out, t_in, t_mlp, sem = refs
    step = pl.program_id(0)

    @pl.when(step == 0)
    def _():
        copies = load_pieces(me_ref, loads, spots, arrays, [w_out, w_in, w_mlp], sem)
        t_out[...] = jnp.zeros_like(t_out)
        t_in[...] = jnp.zeros_like(t_in)
        t_mlp[...] = jnp.zeros_like(t_mlp)
        gain_grad_ref[...] = jnp.zeros_like(gain_grad_ref)
        for copy in copies:
            copy.wait()

    mixed = mix_ref[...]
    cot = cot_ref[...]
    hidden = tokens_ref[...].astype(f32) + dot_nn(mixed, w_out[...])
    hidden_ref[...] = hidden
    normed, scale = norm_of(hidden)
    gain = gain_ref[...]
    normed_mlp = (normed * gain).astype(bf16)
    grad_gated = dot_nt(cot, w_mlp[...])
    entry = dot_nn(normed_mlp, w_in[:, :FF])
    gate = dot_nn(normed_mlp, w_in[:, FF:])
    below = 0.5 * (1.0 + lax.erf(entry * 0.7071067811865476))
    density = jnp.exp(-0.5 * entry * entry) * 0.3989422804014327
    unit = entry * below
    gated = (unit * gate).astype(bf16)
    gated_ref[...] = gated
    grad_entry = ((below + entry * density) * (gate * grad_gated)).astype(bf16)
    grad_gate = (unit * grad_gated).astype(bf16)
    t_mlp[...] += dot_tn(gated, cot)
    turned = normed_mlp.T
    t_in[:, :FF] += dot_nn(turned, grad_entry)
    t_in[:, FF:] += dot_nn(turned, grad_gate)
    grad_normed = dot_nt(grad_entry, w_in[:, :FF]) + dot_nt(grad_gate, w_in[:, FF:])
    gain_grad_ref[...] += jnp.sum(grad_normed * normed, axis=0, keepdims=True)
    grad_hidden = cot.astype(f32) + norm_back(grad_normed * gain, normed, scale)
    grad_hidden_ref[...] = grad_hidden
    grad_out = grad_hidden.astype(bf16)
    t_out[...] += dot_tn(mixed, grad_out)
    grad_mix_ref[...] = dot_nt(grad_out, w_out[...]).astype(bf16)

    @pl.when(step == pl.num_programs(0) - 1)
    def _():
        store_blocks(me_ref, backs[0][0], t_out, out_grads)
        store_blocks(me_ref, backs[1][0], t_in, in_grads)
        store_blocks(me_ref, backs[2][0], t_mlp, mlp_grads)


def backward_kernel(
    spots, outs_n, me_ref, normed_ref, qkv_ref, probs_ref, grad_mix_ref, tables_ref, masks_ref, *refs
):
    grad_ref = refs[0]
    outs = refs[1 : 1 + outs_n]
    total, grad_keys, grad_values = refs[1 + outs_n :]
    step = pl.program_id(0)

    @pl.when(step == 0)
    def _():
        total[...] = jnp.zeros_like(total)

    tables = (tables_ref[0], tables_ref[1], tables_ref[2])

    grad_keys[...] = jnp.zeros_like(grad_keys)
    grad_values[...] = jnp.zeros_like(grad_values)
    turned_grads, turned_keys = [], []
    for pair in range(EACH):
        column = pair * 3 * PAIR + PAIR
        turned_grads.append(grad_mix_ref[:, pair * PAIR : (pair + 1) * PAIR].T)
        turned_keys.append(turned_windows(qkv_ref[:, column : column + PAIR]))
    grad_queries = [[None] * BLOCKS for _ in range(EACH)]

    def soften(pair, block):
        column = pair * 3 * PAIR + 2 * PAIR
        rows = slice(block * BLOCK, (block + 1) * BLOCK)
        window = slice(STARTS[block], STARTS[block] + SPAN)
        return dot_nn(qkv_ref[window, column : column + PAIR], apart(turned_grads[pair][:, rows]))

    def score(pair, block, grad_soft):
        soft = probs_ref[0, 0, pair, block].astype(f32)
        inner = jnp.sum(soft * grad_soft, axis=0, keepdims=True)
        return (soft * (grad_soft - inner)).astype(bf16)

    def spread(pair, block, grad_scores):
        column = pair * 3 * PAIR
        own = slice(pair * PAIR, (pair + 1) * PAIR)
        rows = slice(block * BLOCK, (block + 1) * BLOCK)
        window = slice(STARTS[block], STARTS[block] + SPAN)
        queries = both_heads(qkv_ref[rows, column : column + PAIR], masks_ref)
        grad_mix = both_heads(grad_mix_ref[rows, own], masks_ref)
        grad_values[window, own] += dot_nn(probs_ref[0, 0, pair, block], grad_mix)
        grad_keys[window, own] += dot_nn(grad_scores, queries)
        grad_queries[pair][block] = one_of_each(dot_nn(turned_keys[pair][block], grad_scores))
        if block == BLOCKS - 1:
            turned = jnp.concatenate(grad_queries[pair], axis=1).T * HEAD**-0.5
            grad_ref[:, column : column + PAIR] = turn(turned, tables, -1).astype(bf16)
            grad_ref[:, column + PAIR : column + 2 * PAIR] = turn(grad_keys[:, own], tables, -1).astype(bf16)
            grad_ref[:, column + 2 * PAIR : column + 3 * PAIR] = grad_values[:, own].astype(bf16)

    staggered([(pair, block) for pair in range(EACH) for block in range(BLOCKS)], soften, score, spread)
    total[...] += dot_tn(normed_ref[...], grad_ref[...])

    @pl.when(step == pl.num_programs(0) - 1)
    def _():
        store_blocks(me_ref, spots, total, outs)


def final_kernel(loads, spots, arrays_n, me_ref, tokens_ref, gain_ref, grad_hidden_ref, grad_ref, *refs):
    arrays = refs[:arrays_n]
    tokens_grad_ref, gain_grad_ref, weight, sem = refs[arrays_n:]

    @pl.when(pl.program_id(0) == 0)
    def _():
        copies = load_pieces(me_ref, loads, spots, arrays, [weight], sem)
        gain_grad_ref[...] = jnp.zeros_like(gain_grad_ref)
        for copy in copies:
            copy.wait()

    grad_normed = dot_nt(grad_ref[...], weight[...])
    normed, scale = norm_of(tokens_ref[...].astype(f32))
    gain_grad_ref[...] += jnp.sum(grad_normed * normed, axis=0, keepdims=True)
    tokens_grad_ref[...] = grad_hidden_ref[...] + norm_back(grad_normed * gain_ref[...], normed, scale)


def output_kernel(loads, spots, arrays_n, me_ref, hidden_ref, gated_ref, *refs):
    arrays = refs[:arrays_n]
    output_ref, weight, sem = refs[-3:]

    @pl.when(pl.program_id(0) == 0)
    def _():
        for copy in load_pieces(me_ref, loads, spots, arrays, [weight], sem):
            copy.wait()

    output_ref[...] = (hidden_ref[...] + dot_nn(gated_ref[...], weight[...])).astype(bf16)


SMEM = pl.BlockSpec(memory_space=pltpu.SMEM)
ANYWHERE = pl.BlockSpec(memory_space=pl.ANY)


def rows_spec(rows, columns):
    return pl.BlockSpec((rows, columns), lambda i: (i, 0))


def whole_spec(*shape):
    return pl.BlockSpec(shape, lambda i: (0,) * len(shape))


def call(kernel, steps, inputs, outputs, scratch, flops, nbytes, waits=(), through=(), into=()):
    extra = list(waits) + list(through) + list(into)
    n_in, n_out, n_through = len(inputs), len(outputs), len(through)
    begin = n_in + len(extra)

    def trimmed(*refs):
        kernel(*refs[:n_in], *refs[begin : begin + n_out], *refs[begin + n_out + n_through :])

    aliases = {n_in + len(waits) + at: n_out + at for at in range(n_through)}
    aliases.update({n_in + len(waits) + n_through + at: at for at in range(len(into))})
    results = pl.pallas_call(
        trimmed,
        grid=(steps,),
        in_specs=[spec for _, spec in inputs] + [ANYWHERE] * len(extra),
        out_specs=[spec for _, _, spec in outputs] + [ANYWHERE] * n_through,
        out_shape=[jax.ShapeDtypeStruct(shape, dtype) for shape, dtype, _ in outputs]
        + [jax.ShapeDtypeStruct(array.shape, array.dtype) for array in through],
        scratch_shapes=scratch,
        input_output_aliases=aliases,
        compiler_params=pltpu.CompilerParams(
            dimension_semantics=("arbitrary",), vmem_limit_bytes=VMEM_LIMIT
        ),
        cost_estimate=pl.CostEstimate(flops=int(flops), bytes_accessed=int(nbytes), transcendentals=0),
    )(*[array for array, _ in inputs], *extra)
    if not through:
        return results
    return results[:n_out], results[n_out:]


def rope_constants():
    inverse = 10000.0 ** (-np.arange(0, HEAD, 2, dtype=np.float64) / HEAD)
    angles = np.arange(LEN, dtype=np.float64)[:, None] * inverse[None, :]
    angles = np.concatenate([angles] * 4, axis=-1)
    upper = (np.arange(PAIR) % HEAD >= HEAD // 2)[None, :]
    sine = np.sin(angles)
    return np.stack([np.cos(angles), np.where(upper, sine, 0.0), np.where(upper, 0.0, -sine)]).astype(
        np.float32
    )


def spread_loads(arrays, flips, start, width, weight, column):
    loads, spots = [], []
    for index, blocks, first_chip, other in arrays:
        for block in range(blocks):
            loads.append((index, block, start, width, weight))
            spots.append((flips[first_chip + block], 1, 48, 0, other, width, column))
    return loads, spots


def gather_weights(qkv_weight, out_weight, in_weight, mlp_weight, norm_gains):
    by_pair = qkv_weight.reshape(24, 3, PAIRS, PAIR).transpose(0, 2, 1, 3).reshape(24, PAIRS, 3 * PAIR)
    gain_row = jnp.pad(norm_gains.reshape(1, 48), ((0, 23), (0, 80)))
    early = split_columns(
        jnp.concatenate([by_pair[:, 0], gain_row, by_pair[:, 1], gain_row], axis=1)
    )
    later = split_columns(
        jnp.concatenate([by_pair[:, 2], by_pair[:, 4], by_pair[:, 3], by_pair[:, 5]], axis=1)
    )
    own_in = split_columns(after(in_weight.reshape(24, 2 * FF), early))
    own_out = split_columns(after(out_weight.reshape(24, D), early))
    own_mlp = split_columns(after(mlp_weight.reshape(36, D), early))
    own_mlp = ordered(ALONG_X, own_mlp, swap(own_mlp, ALONG_X), 0)

    line = along_line(early)
    plane = jnp.concatenate([line, swap(line, ALONG_X)])
    far = swap(plane, ALONG_Y)
    first_arrays = [plane, far, swap(plane, CORE), swap(far, CORE)]
    chips = chip_flips(16, ALONG_X, ALONG_Y)
    slots = [(0, 8, 0, 0), (1, 8, 8, 0), (2, 8, 0, 1), (3, 8, 8, 1)]
    first = (first_arrays, *spread_loads(slots, chips, 0, 3 * PAIR, 0, 0))
    scales = jnp.concatenate([plane, far])[:, :, 3 * PAIR : 3 * PAIR + 48]
    scales = jnp.concatenate([scales[:, 0], scales[:, 24]], axis=1)
    held = (lax.axis_index("fsdp") ^ np.asarray(chips, np.int32)) // 2
    spot = held[None, :] == np.arange(16, dtype=np.int32)[:, None]
    gains = dot_nn(spot.astype(bf16), scales).reshape(-1)

    line = along_line(after(later, line))
    early_plane = plane
    plane = jnp.concatenate([line, swap(line, ALONG_Y)])
    far = swap(plane, ALONG_X)
    other_arrays = [plane, far, swap(plane, CORE), swap(far, CORE)]
    chips = chip_flips(16, ALONG_Y, ALONG_X)
    others = [
        (other_arrays, *spread_loads(slots, chips, 3 * PAIR * at, 3 * PAIR, 0, 0)) for at in range(2)
    ]

    rows = own_mlp.shape[0] // 3
    thirds = [own_mlp[rows * i : rows * (i + 1)] for i in range(3)]
    own = after(jnp.concatenate([own_in, own_out] + thirds, axis=1), early_plane)
    start_out, start_mlp = FF, FF + D // 2
    parts = [own] + [swap(own, ALONG_Z * j) for j in (1, 2, 3)]
    rest_arrays = []

    def near(own_mlp):
        thirds = [own_mlp[rows * i : rows * (i + 1)] for i in range(3)]
        own = jnp.concatenate([own_in, own_out] + thirds, axis=1)
        line = jnp.stack([own] + parts[1:])
        beside = swap(line[:, :, :start_out], ALONG_X), swap(line[:, :, start_out:], ALONG_Y)
        return line, line[:, :, :start_mlp], beside

    def far(line, head, beside):
        beside_in, beside_rest = beside
        beside_out = beside_rest[:, :, : D // 2]
        mlp = jnp.concatenate([line[:, :, start_mlp:], beside_rest[:, :, D // 2 :]])
        far_in = swap(jnp.concatenate([head[:, :, :start_out], beside_in]), ALONG_Y)
        far_out = swap(jnp.concatenate([head[:, :, start_out:], beside_out]), ALONG_X)
        return (beside_in, beside_out), (far_in, far_out), mlp, swap(mlp, CORE)

    def across(head, beside, beyond, mlp, mlp_other):
        all_in = jnp.concatenate([head[:, :, :start_out], beside[0], beyond[0]])
        all_out = jnp.concatenate([head[:, :, start_out:], beside[1], beyond[1]])
        both = jnp.concatenate([all_in, all_out], axis=2)
        rest_arrays.extend([both, swap(both, CORE), mlp, mlp_other])

    in_loads, in_spots = spread_loads(
        [(0, 16, 0, 0), (1, 16, 0, 1)], chip_flips(16, ALONG_X, ALONG_Y), 0, FF, 1, 0
    )
    out_loads, out_spots = spread_loads(
        [(0, 16, 0, 0), (1, 16, 0, 1)], chip_flips(16, ALONG_Y, ALONG_X), start_out, D // 2, 0, 0
    )
    mlp_loads, mlp_spots = [], []
    for other in (0, 1):
        for block, flips in enumerate(chip_flips(8, ALONG_Y, 0)):
            for third in range(3):
                mlp_loads.append((2 + other, block, third * (D // 2), D // 2, 2))
                mlp_spots.append((flips, 2, 144, third * 48, other, D // 2, 0))
    rest = (rest_arrays, out_loads + in_loads + mlp_loads, out_spots + in_spots + mlp_spots)

    last_loads, last_spots = list(first[1]), list(first[2])
    for group in range(2):
        column = WIDTH * (group + 1)
        more = spread_loads(slots, chips, 3 * PAIR * group, 3 * PAIR, 0, column)
        last_loads += [(load[0] + 4,) + load[1:] for load in more[0]]
        last_spots += more[1]
    end_loads = [(load[0] - 2,) + load[1:4] + (0,) for load in mlp_loads]
    last = lambda: (first_arrays + other_arrays, last_loads, last_spots)
    ends = lambda: (rest_arrays[2:], end_loads, mlp_spots)
    return gains, [first] + others, rest, last, ends, (own_mlp, parts[1:], near, far, across)


def gather_simply(qkv_weight, out_weight, in_weight, mlp_weight, norm_gains):
    whole = lambda w: lax.all_gather(w, "fsdp", axis=0, tiled=True)
    by_pair = whole(qkv_weight).reshape(D, 3, PAIRS, PAIR).transpose(0, 2, 1, 3)
    w_qkv = by_pair.reshape(1, D, 3 * D)
    w_in, w_out = whole(in_weight).reshape(1, D, 2 * FF), whole(out_weight).reshape(1, D, D)
    w_mlp = whole(mlp_weight).reshape(1, FF, D)
    groups = [([w_qkv], [(0, 0, at * WIDTH, WIDTH, 0)], [NOWHERE]) for at in range(GROUPS)]
    rest = (
        [w_out, w_in, w_mlp],
        [(0, 0, 0, D, 0), (1, 0, 0, 2 * FF, 1), (2, 0, 0, D, 2)],
        [NOWHERE] * 3,
    )
    last = lambda: ([w_qkv], [(0, 0, 0, 3 * D, 0)], [NOWHERE])
    ends = lambda: ([w_mlp], [(0, 0, 0, D, 0)], [NOWHERE])
    return whole(norm_gains), groups, rest, last, ends, None


def shards(devices, tokens, qkv_weight, out_weight, in_weight, mlp_weight, norm_gains, cotangent):
    count = tokens.shape[0]
    sequences = count // LEN
    fast = devices == 32
    gather = gather_weights if fast else gather_simply
    gains, groups, rest, last, ends, rounds = gather(
        qkv_weight, out_weight, in_weight, mlp_weight, norm_gains
    )
    gains = gains.astype(f32)
    gain_attn, gain_mlp = gains[:D].reshape(1, D), gains[D:].reshape(1, D)
    me = lax.axis_index("fsdp").astype(jnp.int32).reshape(1)

    def back_places(rows, columns, first, second):
        if not fast:
            return [NOWHERE], [(1, rows, columns)]
        half = columns // 2
        blocks = 8 if second is None else 16
        rows = rows // blocks
        spots = [
            (flips, 2 if second is None else 1, rows, 0, other, half, 0)
            for other in (0, 1)
            for flips in chip_flips(blocks, first, second or 0)
        ]
        return spots, [(blocks, rows, half)] * 2

    tables = jnp.asarray(rope_constants())
    masks = np.arange(PAIR)[None, :] // HEAD == np.arange(2)[:, None]
    masks = jnp.asarray(masks.astype(np.float32)).astype(bf16)
    probs_shape = (GROUPS, sequences, EACH, BLOCKS, SPAN, SPAN)
    probs_spec = lambda at: pl.BlockSpec((1, 1) + probs_shape[2:], lambda i: (at, i, 0, 0, 0, 0))
    group_spec = lambda at, columns: pl.BlockSpec((LEN, columns), lambda i: (i, at))

    kept = []

    def forward(at, waits, through):
        arrays, loads, spots = groups[at]
        outputs = [
            ((count, 3 * D), bf16, group_spec(at, WIDTH)),
            (probs_shape, bf16, probs_spec(at)),
            ((count, D), bf16, group_spec(at, EACH * PAIR)),
        ]
        if at == 0:
            outputs.append(((count, D), bf16, rows_spec(LEN, D)))
        results = call(
            functools.partial(forward_kernel, loads, spots, len(arrays)),
            sequences,
            [
                (me, SMEM),
                (kept[3] if kept else tokens, rows_spec(LEN, D)),
                (gain_attn, whole_spec(1, D)),
                (tables, whole_spec(3, LEN, PAIR)),
                (masks, whole_spec(2, PAIR)),
            ]
            + [(array, ANYWHERE) for array in arrays],
            outputs,
            [
                pltpu.VMEM((D, WIDTH), bf16),
                pltpu.VMEM((3, SPAN, SPAN), f32),
                pltpu.SemaphoreType.DMA,
            ],
            4 * count * D * WIDTH,
            count * WIDTH * 8,
            waits=waits,
            through=through,
            into=kept[:3],
        )
        results, handed = results if through else (results, [])
        kept[: len(results)] = results
        return handed

    if fast:
        own_mlp, parts, near, far, across = rounds
        (own_mlp,) = forward(0, [], [own_mlp])
        line, head, beside = near(own_mlp)
        (head,) = forward(1, parts, [head])
        beside, beyond, mlp, mlp_other = far(line, head, beside)
        (head,) = forward(2, list(beside), [head])
        across(head, beside, beyond, mlp, mlp_other)
    else:
        for at in range(GROUPS):
            forward(at, [], [])
    qkv, probs, mix, normed = kept

    step_rows = 256
    arrays, loads, spots = rest
    backs = (
        back_places(D, D, ALONG_X, ALONG_Y),
        back_places(D, 2 * FF, ALONG_Y, ALONG_X),
        back_places(FF, D, ALONG_Y, None),
    )
    results = call(
        functools.partial(feed_kernel, loads, spots, len(arrays), backs),
        count // step_rows,
        [(me, SMEM)]
        + [
            (tokens, rows_spec(step_rows, D)),
            (cotangent, rows_spec(step_rows, D)),
            (gain_mlp, whole_spec(1, D)),
        ]
        + [(mix, rows_spec(step_rows, D))]
        + [(array, ANYWHERE) for array in arrays],
        [
            ((count, D), f32, rows_spec(step_rows, D)),
            ((count, FF), bf16, rows_spec(step_rows, FF)),
            ((count, D), f32, rows_spec(step_rows, D)),
        ]
        + [((count, D), bf16, rows_spec(step_rows, D)), ((1, D), f32, whole_spec(1, D))]
        + [(shape, bf16, whole_spec(*shape)) for _, shapes in backs for shape in shapes],
        [
            pltpu.VMEM((D, D), bf16),
            pltpu.VMEM((D, 2 * FF), bf16),
            pltpu.VMEM((FF, D), bf16),
            pltpu.VMEM((D, D), f32),
            pltpu.VMEM((D, 2 * FF), f32),
            pltpu.VMEM((FF, D), f32),
            pltpu.SemaphoreType.DMA,
        ],
        2 * count * (3 * D * D + 8 * D * FF),
        count * D * 16,
    )
    hidden, gated, grad_hidden, grad_mix, gain_mlp_grad = results[:5]
    weight_grads = results[5:]

    grad_blocks = [None] * GROUPS
    grads = []

    def attention_back(at, waits, through):
        order = (ALONG_X, ALONG_Y) if at == 0 else (ALONG_Y, ALONG_X)
        spots, shapes = back_places(D, WIDTH, *order)
        results = call(
            functools.partial(backward_kernel, spots, len(shapes)),
            sequences,
            [
                (me, SMEM),
                (normed, rows_spec(LEN, D)),
                (qkv, group_spec(at, WIDTH)),
                (probs, probs_spec(at)),
                (grad_mix, group_spec(at, EACH * PAIR)),
                (tables, whole_spec(3, LEN, PAIR)),
                (masks, whole_spec(2, PAIR)),
            ],
            [((count, 3 * D), bf16, group_spec(at, WIDTH))]
            + [(shape, bf16, whole_spec(*shape)) for shape in shapes],
            [pltpu.VMEM((D, WIDTH), f32)] + [pltpu.VMEM((LEN, EACH * PAIR), f32)] * 2,
            4 * count * D * WIDTH,
            count * WIDTH * 8,
            waits=waits,
            through=through,
            into=grads,
        )
        results, handed = results if through else (results, [])
        grads[:] = results[:1]
        grad_blocks[at] = results[1:]
        return handed

    last_rows = 256
    halves = 2
    steps = count // last_rows // halves

    def last_part(part, before, waits, through):
        arrays, loads, spots = last()
        part_rows = lambda columns: pl.BlockSpec((last_rows, columns), lambda i: (i + part * steps, 0))
        inputs = (
            [
                (me, SMEM),
                (tokens, part_rows(D)),
                (gain_attn, whole_spec(1, D)),
                (grad_hidden, part_rows(D)),
                (grads[0], part_rows(3 * D)),
            ]
            + [(array, ANYWHERE) for array in arrays]
        )
        return call(
            functools.partial(final_kernel, loads, spots, len(arrays)),
            steps,
            inputs,
            [((count, D), f32, part_rows(D)), ((1, D), f32, whole_spec(1, D))],
            [pltpu.VMEM((D, 3 * D), bf16), pltpu.SemaphoreType.DMA],
            6 * count * D * D // halves,
            count * D * 20 // halves,
            waits=waits,
            through=through,
            into=before,
        )

    def layer_output(waits, through):
        arrays, loads, spots = ends()
        return call(
            functools.partial(output_kernel, loads, spots, len(arrays)),
            count // last_rows,
            [(me, SMEM), (hidden, rows_spec(last_rows, D)), (gated, rows_spec(last_rows, FF))]
            + [(array, ANYWHERE) for array in arrays],
            [((count, D), bf16, rows_spec(last_rows, D))],
            [pltpu.VMEM((FF, D), bf16), pltpu.SemaphoreType.DMA],
            2 * count * FF * D,
            count * D * 12,
            waits=waits,
            through=through,
        )

    if fast:
        (out_keep, out_send), (in_keep, in_send), (mlp_keep, mlp_send) = (
            weight_grads[:2],
            weight_grads[2:4],
            weight_grads[4:],
        )
        out_got, in_got, mlp_got = swap(out_send, CORE), swap(in_send, CORE), swap(mlp_send, CORE)
        in_keep, out_keep, mlp_keep = attention_back(2, [], [in_keep, out_keep, mlp_keep])
        in_keep, in_send = halved(in_keep, in_got)
        out_keep, out_send = halved(out_keep, out_got)
        mlp_keep, mlp_send = halved(mlp_keep, mlp_got)
        in_got, out_got, mlp_got = swap(in_send, ALONG_X), swap(out_send, ALONG_Y), swap(mlp_send, ALONG_Y)
        in_keep, out_keep, mlp_keep = attention_back(1, [], [in_keep, out_keep, mlp_keep])
        in_keep, in_send = halved(in_keep, in_got)
        out_keep, out_send = halved(out_keep, out_got)
        mlp_line = joined_sum(mlp_keep, mlp_got)
        in_got, out_got = swap(in_send, ALONG_Y), swap(out_send, ALONG_X)
        mlp_got = [swap(mlp_line[j], ALONG_Z * j) for j in (1, 2, 3)]
        later_got = [swap(grad_blocks[at][1], CORE) for at in (1, 2)]
        in_keep, out_keep, mlp_own, *later = attention_back(
            0, [mlp_line], [in_keep, out_keep, mlp_line[0], grad_blocks[1][0], grad_blocks[2][0]]
        )
        line = jnp.concatenate([joined_sum(in_keep, in_got), joined_sum(out_keep, out_got)], axis=2)
        line_got = [swap(line[j], ALONG_Z * j) for j in (1, 2, 3)]
        later = [halved(kept, got) for kept, got in zip(later, later_got)]
        later_keep = jnp.concatenate([keep for keep, _ in later], axis=2)
        later_got = swap(jnp.concatenate([send for _, send in later], axis=2), ALONG_X)
        early_got = swap(grad_blocks[0][1], CORE)
        total_mlp = mlp_own.astype(f32)
        for got in mlp_got:
            total_mlp = total_mlp + got.astype(f32)
        rows = total_mlp.shape[0] // 2
        low, high = total_mlp[:rows], total_mlp[rows:]
        mlp_other = swap(jnp.where(bit_of(ALONG_X), low, high).astype(bf16), ALONG_X)
        mlp_own = jnp.where(bit_of(ALONG_X), high, low)
        (tokens_grad, gain_first), (later_keep, early_keep) = last_part(
            0, [], [], [later_keep, grad_blocks[0][0]]
        )
        later_keep, later_send = halved(later_keep, later_got)
        later_got = swap(later_send, ALONG_Y)
        early_keep, early_send = halved(early_keep, early_got)
        early_got = swap(early_send, ALONG_Y)
        (tokens_grad, gain_last), (later_keep, early_keep) = last_part(
            1, [tokens_grad], [], [later_keep, early_keep]
        )
        gains_grad = jnp.concatenate([(gain_first + gain_last).reshape(-1), gain_mlp_grad.reshape(-1)])
        gains_keep, gains_got = swap_half(gains_grad, 2 * ALONG_Z)
        early_keep, early_send = halved(early_keep, early_got)
        early_got = swap(early_send, ALONG_X)
        later_line = joined_sum(later_keep, later_got)
        (output,), (early_keep, line_own, mlp_own) = layer_output(
            [later_line], [early_keep, line[0], mlp_own]
        )
        total = line_own.astype(f32)
        for got in line_got:
            total = total + got.astype(f32)
        total_mlp = mlp_own + mlp_other.astype(f32)
        joined_mlp = join_columns(total_mlp)
        joined_rest = join_columns(total)
        early_line = joined_sum(early_keep, early_got)
        gains_share = after(gains_keep + gains_got, early_line)
        for bits in (ALONG_Z, ALONG_Y, ALONG_X, CORE):
            gains_keep, gains_got = swap_half(gains_share, bits)
            gains_share = gains_keep + gains_got
        early_later = summed_line(jnp.concatenate([early_line, later_line], axis=2))
        mlp_share = both_columns(joined_mlp, 0, D // 2).reshape(-1)
        in_share = both_columns(joined_rest, 0, FF).reshape(-1)
        out_share = both_columns(joined_rest, FF, FF + D // 2).reshape(-1)
        joined = join_columns(early_later)
        qkv_share = [both_columns(joined, at * 3 * PAIR, (at + 1) * 3 * PAIR) for at in range(GROUPS)]
        qkv_share = jnp.concatenate(qkv_share, axis=1).reshape(24, PAIRS, 3, PAIR)
        qkv_share = qkv_share.transpose(0, 2, 1, 3).reshape(-1)
    else:
        for at in reversed(range(GROUPS)):
            attention_back(at, [], [])
        tokens_grad, gain_first = last_part(0, [], [], [])
        tokens_grad, gain_last = last_part(1, [tokens_grad], [], [])
        (output,) = layer_output([], [])
        add = lambda grad: lax.psum_scatter(
            grad.astype(f32).reshape(-1), "fsdp", scatter_dimension=0, tiled=True
        )
        out_share, in_share, mlp_share = (add(grad) for grad in weight_grads)
        qkv_grad = jnp.concatenate([blocks[0].reshape(D, EACH, 3, PAIR) for blocks in grad_blocks], axis=1)
        qkv_share = add(qkv_grad.transpose(0, 2, 1, 3))
        gains_share = add(jnp.concatenate([gain_first + gain_last, gain_mlp_grad]))
    return (output, tokens_grad, qkv_share, out_share, in_share, mlp_share, gains_share)


def solution(mesh):
    placed = (P("fsdp", None),) + (P("fsdp"),) * 5 + (P("fsdp", None),)
    return jax.shard_map(
        functools.partial(shards, mesh.shape["fsdp"]),
        mesh=mesh,
        in_specs=placed,
        out_specs=(P("fsdp", None),) * 2 + (P("fsdp"),) * 5,
        check_vma=False,
    )
```
